512 devices in a mesh: sec: 32 (over y_hi, z), tile: 16 (over y_lo, x, core).
Axes of the slice: x: 4, y: 4 (y_hi: 2, y_lo: 2; y = y_hi * 2 + y_lo), z: 16, core: 2. Of those that a mesh axis runs over, the one named last changes fastest.
Arguments:
- image: bfloat16 [32, 4096, 1024], P('sec', 'tile'), may hold values from -6 to 6
- weight: bfloat16 [32, 4096, 1024], P('sec', 'tile'), may hold values from 0.25 to 4
- lens_filter_taps: float32 [32, 16, 25], P('sec', 'tile'), may hold values from -2 to 2
- block_src: int32 [32, 16, 16, 2], P('sec', 'tile'), may hold values from 0 to 15
- block_dst: int32 [32, 16, 16, 2], P('sec', None, 'tile'), may hold values from 0 to 15, as said below
- valid_count: int32 [32, 16, 16], P('sec', 'tile'), may hold values from 1 to 2, as said below
- anchor: bfloat16 [256, 128, 128], P('tile'), may hold values from -6 to 6
Outputs:
- correlation: float32 [32, 512, 128, 128], P('sec', 'tile')
The draws below stay inside these ranges and needn't reach their ends.
Inputs may be any that keep to these rules, and one draw needn't show every extreme that they name: `block_dst`: every block of every strip receives at least one live slot. `valid_count`: in every section some strip receives 2 live slots from every tile; block_src and block_dst are 0 in slots at or beyond the valid count.
All inputs are finite; a program needn't handle non-finite values.
Results may differ from the reference program's by a relative error of at most 0.02.
Values may be sent and summed in bfloat16 or wider, within the bound.
No kernel may reach another device: no remote copies, remote signals or barrier semaphores. Data moves between devices by JAX's collectives and lax.ppermute only.
A program may use at most 64 MiB of HBM per device.

```python
import math
import jax
import jax.numpy as jnp
from jax import lax

B = 128
CAP = 2
TH = 256
TW = 1024
TB = 16
SB = 16
SECTION_COUNT = 32
TILES = 16
ROWS = 4096


def placement_lists(key):
    pieces = jax.random.split(jax.random.fold_in(key, 7), 5)
    counts = jax.random.randint(pieces[0], (SECTION_COUNT, TILES, TILES), 1, CAP + 1)
    hot_strip = jax.random.randint(pieces[1], (SECTION_COUNT,), 0, TILES)
    is_hot = jnp.arange(TILES)[None, None, :] == hot_strip[:, None, None]
    counts = jnp.where(is_hot, CAP, counts).astype(jnp.int32)
    source_ids = jax.random.randint(pieces[2], (SECTION_COUNT, TILES, TILES, CAP), 0, TB)
    dest_ids = jax.random.randint(pieces[3], (SECTION_COUNT, TILES, TILES, CAP), 0, SB)
    offsets = jax.random.randint(pieces[4], (SECTION_COUNT,), 0, SB)
    tile_index = jnp.arange(TILES, dtype=jnp.int32)
    first_dest = (tile_index[None, :, None] + tile_index[None, None, :] + offsets[:, None, None]) % SB
    is_first = jnp.arange(CAP)[None, None, None, :] == 0
    dest_ids = jnp.where(is_first, first_dest[..., None], dest_ids)
    is_live = jnp.arange(CAP)[None, None, None, :] < counts[..., None]
    source_ids = jnp.where(is_live, source_ids, 0).astype(jnp.int32)
    dest_ids = jnp.where(is_live, dest_ids, 0).astype(jnp.int32)
    return (source_ids, dest_ids, counts)


def draw_block_src(key, part):
    return placement_lists(key)[0]


def draw_block_dst(key, part):
    return placement_lists(key)[1]


def draw_valid_count(key, part):
    return placement_lists(key)[2]


def steps_of(rng, dims, cuts, smallest, largest):
    def one(axis_at, blocks):
        draws = jax.random.uniform(jax.random.fold_in(jax.random.fold_in(rng, 6), axis_at), (blocks,), jnp.float32, smallest / len(cuts), largest / len(cuts))
        return jnp.repeat(jnp.exp(draws), dims[axis_at] // blocks).reshape((-1,) + (1,) * (len(dims) - axis_at - 1))

    factor_of = one(*cuts[0])
    for cut in cuts[1:]:
        factor_of = factor_of * one(*cut)
    return factor_of


def normal_values(stream_key, dims, width, most, cuts=(), kind=jnp.bfloat16):
    values = width * jax.random.normal(stream_key, dims, jnp.float32)
    if cuts:
        values = values * steps_of(stream_key, dims, cuts, -0.22, 0.18)
    return jnp.clip(values, -most, most).astype(kind)


def setup_inputs(seed: int = 0) -> dict:
    key_list = jax.random.split(jax.random.key(seed), 8)
    return {
        "image": normal_values(key_list[0], (SECTION_COUNT, ROWS, TW), 1.0, 6.0, ((0, 32), (1, 16))),
        "weight": jnp.clip(jnp.exp(math.log(4.0) - 2.7725887 * jax.random.uniform(key_list[1], (SECTION_COUNT, ROWS, TW), jnp.float32) ** steps_of(key_list[1], (SECTION_COUNT, ROWS, TW), ((0, 32), (1, 16)), -0.2, 0.2)), 0.25, 4.0).astype(jnp.bfloat16),
        "lens_filter_taps": normal_values(key_list[2], (SECTION_COUNT, TILES, 25), 0.4, 2.0, ((0, 32), (1, 16)), jnp.float32),
        "block_src": draw_block_src(jax.random.fold_in(key_list[7], 71), 0),
        "block_dst": draw_block_dst(jax.random.fold_in(key_list[7], 71), 0),
        "valid_count": draw_valid_count(jax.random.fold_in(key_list[7], 71), 0),
        "anchor": normal_values(key_list[6], (TILES * SB, B, B), 1.0, 6.0, ((0, 16),)),
    }


def render_section(operands):
    section_image, section_weight, kernel_taps, source_ids, dest_ids, counts = operands
    rows_total = section_image.shape[0]
    padded = jnp.pad(section_image, 2)
    row_taps = jnp.repeat(kernel_taps, TH, axis=0)
    corrected = jnp.zeros((rows_total, TW), jnp.float32)
    for row_off in range(5):
        for col_off in range(5):
            corrected = corrected + row_taps[:, row_off * 5 + col_off][:, None] * padded[row_off:row_off + rows_total, col_off:col_off + TW].astype(jnp.float32)
    weighted = (corrected * section_weight.astype(jnp.float32)).astype(jnp.bfloat16)
    tile_blocks = weighted.reshape(TILES, TH // B, B, TW // B, B).transpose(0, 1, 3, 2, 4).reshape(TILES, TB, B, B)
    picked = tile_blocks[jnp.arange(TILES)[:, None, None], source_ids]
    is_live = jnp.arange(CAP)[None, None, :] < counts[:, :, None]
    picked = jnp.where(is_live[..., None, None], picked, jnp.zeros_like(picked))
    indicator_vector = ((dest_ids[..., None] == jnp.arange(SB)[None, None, None, :]) & is_live[..., None]).astype(jnp.float32)
    strips = jnp.einsum('tdcs,tdcxy->dsxy', indicator_vector, picked.astype(jnp.float32))
    return strips.reshape(TILES * SB, B, B).astype(jnp.bfloat16)

def window_set(strips):
    extended = jnp.concatenate([strips, jnp.zeros_like(strips[:1])], 0)
    aligned = extended[:-1]
    half_shift = jnp.concatenate([extended[:-1, :, B // 2:], extended[1:, :, :B // 2]], 2)
    return jnp.stack([aligned, half_shift], 1).reshape(-1, B, B)

def exact_table(table):
    high = table.astype(jnp.bfloat16)
    low = (table - high.astype(jnp.float32)).astype(jnp.bfloat16)
    return high.astype(jnp.float32) + low.astype(jnp.float32)

def base_tables():
    positions = jnp.arange(B, dtype=jnp.int32)
    product = positions[:, None] * positions[None, :] % B
    angle = product.astype(jnp.float32) * (2.0 * math.pi / B)
    return (jnp.cos(angle), jnp.sin(angle))

def to_half(values):
    return lax.optimization_barrier(values.astype(jnp.bfloat16)).astype(jnp.float32)

def right_mult(data, table):
    return jnp.einsum('wjk,kl->wjl', data, table, precision=lax.Precision.HIGHEST)

def left_mult(table, data):
    return jnp.einsum('jk,wkl->wjl', table, data, precision=lax.Precision.HIGHEST)

def forward(windows):
    cosine, sine_table = base_tables()
    pair_right = exact_table(jnp.concatenate([cosine, sine_table], 1))
    pair_left = exact_table(jnp.concatenate([cosine, sine_table], 0))
    right = to_half(right_mult(windows.astype(jnp.float32), pair_right))
    from_cos = left_mult(pair_left, right[:, :, :B])
    from_sin = left_mult(pair_left, right[:, :, B:])
    spec_re = from_cos[:, :B] - from_sin[:, B:]
    spec_im = -(from_cos[:, B:] + from_sin[:, :B])
    return (spec_re, spec_im)

def correlate(operands):
    current, earlier = operands
    cur_re, cur_im = forward(window_set(current))
    pre_re, pre_im = forward(window_set(earlier))
    cross_re = cur_re * pre_re + cur_im * pre_im
    cross_im = cur_im * pre_re - cur_re * pre_im
    magnitude = jnp.sqrt(cross_re * cross_re + cross_im * cross_im)
    mean_mag = lax.optimization_barrier(jnp.mean(magnitude, axis=(1, 2), keepdims=True))
    denominator = magnitude + 0.1 * mean_mag + 1e-06
    whitened = to_half(jnp.concatenate([cross_re / denominator, cross_im / denominator], 2))
    cosine, sine_table = base_tables()
    inverse_right = exact_table(jnp.concatenate([jnp.concatenate([cosine, sine_table], 1), jnp.concatenate([-sine_table, cosine], 1)], 0))
    inverse_left = exact_table(jnp.concatenate([cosine, -sine_table], 1))
    rows_both = to_half(right_mult(whitened, inverse_right))
    stacked = jnp.concatenate([rows_both[:, :, :B], rows_both[:, :, B:]], 1)
    return (left_mult(inverse_left, stacked) / B).astype(jnp.float32)

def reference(image, weight, lens_filter_taps, block_src, block_dst, valid_count, anchor):
    gathered_strip_list = lax.map(render_section, (image, weight, lens_filter_taps, block_src, block_dst, valid_count))
    earlier = jnp.concatenate([anchor[None], gathered_strip_list[:-1]], 0)
    return lax.map(correlate, (gathered_strip_list, earlier))
```

```python
import jax
import jax.numpy as jnp
import numpy as np
from jax import lax
from jax.experimental import pallas as pl
from jax.experimental.pallas import tpu as pltpu
from jax.sharding import PartitionSpec as P

B = 128
H = B // 2
EDGE = 16
HALF = 8
F32 = jnp.float32
BF16 = jnp.bfloat16
VMEM_LIMIT = 48 * 2**20


def tables():
    j = np.arange(B)
    angle = (j[:, None] * j[None, :] % B) * (2.0 * np.pi / B)
    c, s = np.cos(angle), np.sin(angle)
    right = np.zeros((2 * B, 2 * B))
    for half, start in ((0, 0), (1, H)):
        right[start : start + B, half * H : half * H + H] = c[:, :H]
        right[start : start + B, B + half * H : B + half * H + H] = s[:, :H]
    left = np.block([[c, -s], [-s, -c]])
    q = np.arange((HALF + 1) * B)
    sign = 1.0 - 2.0 * (q % 2)
    middle = np.zeros(((HALF + 1) * B, B))
    for m in range(HALF):
        middle[:, m] = sign * (q // B == m)
        middle[:, H + m] = sign * ((q - H) // B == m)
    back_left = np.block([[c, -s], [s, c]])
    twice = np.where(j[:H] == 0, 1.0, 2.0)[:, None] / B
    back_right = np.zeros((2 * B, 2 * B))
    imag = -twice * s[:H]
    imag[0] = (1.0 - 2.0 * (j % 2)) / B
    for half in range(2):
        lanes = slice(half * B, half * B + B)
        back_right[half * H : half * H + H, lanes] = twice * c[:H]
        back_right[B + half * H : B + half * H + H, lanes] = imag
    return tuple(np.asarray(t, np.float32).astype(BF16) for t in (right, left, middle, back_left, back_right))


def dot(a, b):
    return jnp.dot(a, b, preferred_element_type=F32)


def shifted(x, off):
    rows = x.shape[0]
    if off == 0:
        return x
    gap = jnp.zeros((rows, abs(off)), x.dtype)
    if off > 0:
        return jnp.concatenate([x[:, off:], gap], 1)
    return jnp.concatenate([gap, x[:, :off]], 1)


def banded(taps_ref, which, valid):
    high, low = [], []
    for b in range(5):
        band = jnp.zeros(which.shape, F32)
        for a in range(5):
            band = jnp.where(which == a, taps_ref[0, 0, 5 * a + b], band)
        if valid is not None:
            band = jnp.where(valid, band, 0.0)
        top = band.astype(BF16)
        high.append(top)
        low.append((band - top.astype(F32)).astype(BF16))
    return jnp.concatenate([jnp.concatenate(high, 1), jnp.concatenate(low, 1)], 0)


def lens_kernel(taps_ref, x_ref, weight_ref, blocks_ref, edge_ref):
    x = x_ref[0]
    rows = x.shape[0]
    i = lax.broadcasted_iota(jnp.int32, (rows, rows), 0)
    j = lax.broadcasted_iota(jnp.int32, (rows, rows), 1)
    bands = banded(taps_ref, j - i + 2, None)
    stack = jnp.concatenate([shifted(x, b - 2) for b in range(5)], 0)
    both = dot(bands, stack)
    corrected = both[:rows] + both[rows:]
    edge_ref[:EDGE] = corrected[:EDGE]
    edge_ref[EDGE:] = corrected[rows - EDGE :]
    weighted = (corrected * weight_ref[0].astype(F32)).astype(BF16)
    across = x.shape[1] // B
    for k in range(blocks_ref.shape[0]):
        r, c = k // across * B, k % across * B
        blocks_ref[k] = weighted[r : r + B, c : c + B]


def pick_kernel(taps_ref, src_ref, count_ref, low_ref, high_ref, edge_ref, wtop_ref, wbot_ref, blocks_ref, out_ref, fix_ref):
    e = lax.broadcasted_iota(jnp.int32, (2 * EDGE, 2 * EDGE), 0)
    k = lax.broadcasted_iota(jnp.int32, (2 * EDGE, 2 * EDGE), 1)
    upper = (e < EDGE) & (k < EDGE)
    lower = (e >= EDGE) & (k >= EDGE)
    which = jnp.where(upper, k - (EDGE - 2) - e, k + (EDGE + 2) - e)
    bands = banded(taps_ref, which, upper | lower)
    rim = jnp.concatenate([low_ref[...], high_ref[...]], 0)
    stack = jnp.concatenate([shifted(rim, b - 2) for b in range(5)], 0)
    both = dot(bands, stack)
    corrected = edge_ref[...] + (both[: 2 * EDGE] + both[2 * EDGE :])
    top = (corrected[:EDGE] * wtop_ref[0].astype(F32)).astype(BF16)
    bottom = (corrected[EDGE:] * wbot_ref[0].astype(F32)).astype(BF16)
    count = blocks_ref.shape[0]
    across = count // 2
    for c in range(across):
        fix_ref[c] = top[:, c * B : c * B + B]
        fix_ref[across + c] = bottom[:, c * B : c * B + B]
    for d in range(out_ref.shape[0]):
        for q in range(out_ref.shape[1]):
            live = q < count_ref[0, 0, d]
            s = src_ref[0, 0, d, q]
            zero = jnp.zeros((), BF16)
            out_ref[d, q] = jnp.where(live, blocks_ref[s], zero)
            at = pl.multiple_of(jnp.where(s < across, 0, B - EDGE), EDGE)
            out_ref[d, q, pl.ds(at, EDGE), :] = jnp.where(live, fix_ref[s], zero)


def strip_kernel(dst_ref, in_ref, a_ref, b_ref, first_ref, acc_ref):
    acc_ref[...] = jnp.zeros_like(acc_ref)
    for d in range(in_ref.shape[0]):
        for q in range(in_ref.shape[1]):
            j = dst_ref[0, d, 0, q]
            acc_ref[j] = acc_ref[j] + in_ref[d, q].astype(F32)
    a_ref[...] = acc_ref[: HALF + 1].astype(BF16)
    b_ref[...] = acc_ref[HALF + 1 :].astype(BF16)
    first_ref[0] = acc_ref[0].astype(BF16)


def forward(blocks, right, left, middle):
    spectra = []
    for m in range(HALF):
        p = dot(jnp.concatenate([blocks[m], blocks[m + 1]], 1), right).astype(BF16)
        spectra.append(dot(left, jnp.concatenate([p[:, :B], p[:, B:]], 0)))
    p = dot(jnp.concatenate(blocks, 1), middle).astype(BF16)
    spectra.append(dot(left[:, :B], p))
    return spectra


def current_kernel(a_ref, b_ref, rim_ref, right_ref, left_ref, middle_ref, out_ref):
    blocks = [a_ref[m] for m in range(HALF + 1)] + [b_ref[m] for m in range(HALF - 1)] + [rim_ref[0]]
    for part in range(2):
        spectra = forward(blocks[part * HALF : part * HALF + HALF + 1], right_ref[...], left_ref[...], middle_ref[...])
        for m, f in enumerate(spectra):
            out_ref[part, m] = f.astype(BF16)


def correlate_chunk(cur_ref, part, blocks, right, left, middle, back_left, back_right, out_ref, cross_ref, mag_ref):
    lane = lax.broadcasted_iota(jnp.int32, (1, B), 1)
    twice = jnp.where(lane % H == 0, 1.0, 2.0)
    sums = []
    for m, f in enumerate(forward(blocks, right, left, middle)):
        c = cur_ref[part, m].astype(F32)
        ar, ai, br, bi = c[:B], c[B:], f[:B], f[B:]
        re = ar * br + ai * bi
        im = ai * br - ar * bi
        square = re * re + im * im
        mag = square * lax.rsqrt(jnp.maximum(square, 1e-30))
        cross_ref[m, :B] = re
        cross_ref[m, B:] = im
        mag_ref[m] = mag
        total = jnp.sum(mag, axis=0, keepdims=True)
        sums.append(total * twice if m < HALF else total)
    row = lax.broadcasted_iota(jnp.int32, (HALF, B), 0)
    lanes = lax.broadcasted_iota(jnp.int32, (HALF, B), 1)
    mine = row == lanes % H
    table = jnp.concatenate(sums[:HALF], 0) + jnp.where(mine, sums[HALF], 0.0)
    aligned = lanes < H
    first = jnp.sum(jnp.where(aligned, table, 0.0), axis=1, keepdims=True)
    second = jnp.sum(jnp.where(aligned, 0.0, table), axis=1, keepdims=True)
    floor = jnp.where(aligned, first, second) * (0.1 / (B * B)) + 1e-6
    floor_middle = jnp.sum(jnp.where(mine, floor, 0.0), axis=0, keepdims=True)
    floor_middle = jnp.where(lane % H < HALF, floor_middle, 1.0)

    def whitened(m, low):
        scale = 1.0 / (mag_ref[m] + low)
        return jnp.concatenate([cross_ref[m, :B] * scale, cross_ref[m, B:] * scale], 0).astype(BF16)

    y_middle = dot(back_left[:B], whitened(HALF, floor_middle))
    is_zero = lane % H == 0
    for m in range(HALF):
        y = dot(back_left, whitened(m, floor[m : m + 1]))
        turned = y_middle if m == 0 else pltpu.roll(y_middle, B - m, 1)
        imag = jnp.where(is_zero, turned, y[B:])
        result = dot(jnp.concatenate([y[:B].astype(BF16), imag.astype(BF16)], 1), back_right)
        out_ref[0, 2 * m] = result[:, :B]
        out_ref[0, 2 * m + 1] = result[:, B:]


def first_half_kernel(cur_ref, a_ref, anchor_ref, right, left, middle, back_left, back_right, out_ref, cross_ref, mag_ref):
    is_first = lax.axis_index("sec") == 0
    blocks = [jnp.where(is_first, anchor_ref[m], a_ref[m]) for m in range(HALF + 1)]
    correlate_chunk(cur_ref, 0, blocks, right[...], left[...], middle[...], back_left[...], back_right[...], out_ref, cross_ref, mag_ref)


def second_half_kernel(
    held_ref, cur_ref, a_ref, b_ref, rim_ref, anchor_ref, border_ref, right, left, middle, back_left, back_right, out_ref, cross_ref, mag_ref
):
    del held_ref
    is_first = lax.axis_index("sec") == 0
    blocks = [jnp.where(is_first, anchor_ref[HALF], a_ref[HALF])]
    blocks += [jnp.where(is_first, anchor_ref[HALF + 1 + m], b_ref[m]) for m in range(HALF - 1)]
    blocks += [jnp.where(is_first, border_ref[0], rim_ref[0])]
    correlate_chunk(cur_ref, 1, blocks, right[...], left[...], middle[...], back_left[...], back_right[...], out_ref, cross_ref, mag_ref)


SMEM = pl.BlockSpec(memory_space=pltpu.SMEM)
VMEM = pl.BlockSpec(memory_space=pltpu.VMEM)
ANY = pl.BlockSpec(memory_space=pl.ANY)


def call(kernel, out_shape, in_specs, out_specs, scratch, flops, moved, args, aliases=None, grid=None):
    extra = {} if grid is None else {"grid": grid}
    return pl.pallas_call(
        kernel,
        out_shape=out_shape,
        in_specs=in_specs,
        out_specs=out_specs,
        scratch_shapes=scratch,
        input_output_aliases=aliases or {},
        compiler_params=pltpu.CompilerParams(vmem_limit_bytes=VMEM_LIMIT),
        cost_estimate=pl.CostEstimate(flops=flops, bytes_accessed=moved, transcendentals=0),
        **extra,
    )(*args)


def body(image, weight, lens_filter_taps, block_src, block_dst, valid_count, anchor):
    rows, cols = image.shape[1:]
    strips = lax.axis_size("tile")
    sections = lax.axis_size("sec")
    slots = block_src.shape[-1]
    shape = jax.ShapeDtypeStruct
    forth = [(i, i + 1) for i in range(strips - 1)]
    back = [(i + 1, i) for i in range(strips - 1)]
    low = lax.ppermute(image[0, rows - EDGE :], "tile", forth)
    high = lax.ppermute(image[0, :EDGE], "tile", back)
    tile_blocks = rows // B * (cols // B)
    blocks, edge = call(
        lens_kernel,
        (shape((tile_blocks, B, B), BF16), shape((2 * EDGE, cols), F32)),
        [SMEM, VMEM, VMEM],
        (VMEM, VMEM),
        [],
        2 * 10 * rows * rows * cols,
        3 * 2 * rows * cols,
        (lens_filter_taps, image, weight),
    )
    edge_of = lambda index: pl.BlockSpec((1, EDGE, cols), lambda i: (0, index, 0))
    whole = lambda *dims: pl.BlockSpec(dims, lambda i: (0,) * len(dims))
    outgoing = call(
        pick_kernel,
        shape((strips, slots, B, B), BF16),
        [
            SMEM,
            SMEM,
            SMEM,
            whole(EDGE, cols),
            whole(EDGE, cols),
            whole(2 * EDGE, cols),
            edge_of(0),
            edge_of(rows // EDGE - 1),
            whole(tile_blocks, B, B),
        ],
        whole(strips, slots, B, B),
        [pltpu.VMEM((tile_blocks, EDGE, B), BF16)],
        2**20,
        4 * 2 * rows * cols,
        (lens_filter_taps, block_src, valid_count, low, high, edge, weight, weight, blocks),
        grid=(1,),
    )
    incoming = lax.all_to_all(outgoing, "tile", split_axis=0, concat_axis=0, tiled=True)
    border = lax.ppermute(anchor[:1], "tile", back)
    count = anchor.shape[0]
    part_a, part_b, first = call(
        strip_kernel,
        (shape((HALF + 1, B, B), BF16), shape((HALF - 1, B, B), BF16), shape((1, B, B), BF16)),
        [SMEM, VMEM],
        (VMEM, VMEM, VMEM),
        [pltpu.VMEM((count, B, B), F32)],
        2**20,
        4 * 2 * rows * cols,
        (block_dst, incoming),
    )
    on = [(i, i + 1) for i in range(sections - 1)]
    prior_a = lax.ppermute(part_a, "sec", on)
    prior_b = lax.ppermute(part_b, "sec", on)
    own_rim = lax.ppermute(first, "tile", back)
    across = [(s * strips + d + 1, (s + 1) * strips + d) for s in range(sections - 1) for d in range(strips - 1)]
    prior_rim = lax.ppermute(first, ("sec", "tile"), across)
    right, left, middle, back_left, back_right = (jnp.asarray(t) for t in tables())
    spectra = call(
        current_kernel,
        shape((2, HALF + 1, 2 * B, B), BF16),
        [VMEM] * 6,
        VMEM,
        [],
        2 * 16 * count * B**3,
        8 * count * B * B,
        (part_a, part_b, own_rim, right, left, middle),
    )
    windows = 2 * count
    scratch = [pltpu.VMEM((HALF + 1, 2 * B, B), F32), pltpu.VMEM((HALF + 1, B, B), F32)]
    half = lambda at: pl.BlockSpec((1, windows // 2, B, B), lambda i: (0, at, 0, 0))
    result = shape((1, windows, B, B), F32)
    t_specs = [whole(2 * B, 2 * B)] * 2 + [whole((HALF + 1) * B, B)] + [whole(2 * B, 2 * B)] * 2
    cur_spec = whole(2, HALF + 1, 2 * B, B)
    held = call(
        first_half_kernel,
        result,
        [cur_spec, whole(HALF + 1, B, B), whole(count, B, B)] + t_specs,
        half(0),
        scratch,
        2 * 16 * count * B**3,
        12 * count * B * B,
        (spectra, prior_a, anchor, right, left, middle, back_left, back_right),
        grid=(1,),
    )
    return call(
        second_half_kernel,
        result,
        [ANY, cur_spec, whole(HALF + 1, B, B), whole(HALF - 1, B, B), whole(1, B, B), whole(count, B, B), whole(1, B, B)] + t_specs,
        half(1),
        scratch,
        2 * 16 * count * B**3,
        12 * count * B * B,
        (held, spectra, prior_a, prior_b, prior_rim, anchor, border, right, left, middle, back_left, back_right),
        aliases={0: 0},
        grid=(1,),
    )


def solution(mesh):
    in_specs = (
        P("sec", "tile", None),
        P("sec", "tile", None),
        P("sec", "tile", None),
        P("sec", "tile", None, None),
        P("sec", None, "tile", None),
        P("sec", "tile", None),
        P("tile", None, None),
    )
    out_specs = P("sec", "tile", None, None)
    return jax.shard_map(body, mesh=mesh, in_specs=in_specs, out_specs=out_specs, check_vma=False)
```

```python
import jax
import jax.numpy as jnp
import numpy as np
from jax import lax
from jax.experimental import pallas as pl
from jax.experimental.pallas import tpu as pltpu
from jax.sharding import PartitionSpec as P

B = 128
H = B // 2
EDGE = 16
HALF = 8
F32 = jnp.float32
BF16 = jnp.bfloat16
VMEM_LIMIT = 48 * 2**20
PREPARE_VMEM_LIMIT = 54912 * 2**10


def tables():
    j = np.arange(B)
    angle = (j[:, None] * j[None, :] % B) * (2.0 * np.pi / B)
    c, s = np.cos(angle), np.sin(angle)
    right = np.zeros((2 * B, 2 * B))
    for half, start in ((0, 0), (1, H)):
        right[start : start + B, half * H : half * H + H] = c[:, :H]
        right[start : start + B, B + half * H : B + half * H + H] = s[:, :H]
    left = np.block([[c, -s], [-s, -c]])
    q = np.arange((HALF + 1) * B)
    sign = 1.0 - 2.0 * (q % 2)
    middle = np.zeros(((HALF + 1) * B, B))
    for m in range(HALF):
        middle[:, m] = sign * (q // B == m)
        middle[:, H + m] = sign * ((q - H) // B == m)
    back_left = np.block([[c, -s], [s, c]])
    twice = np.where(j[:H] == 0, 1.0, 2.0)[:, None] / B
    back_right = np.zeros((2 * B, 2 * B))
    imag = -twice * s[:H]
    imag[0] = (1.0 - 2.0 * (j % 2)) / B
    for half in range(2):
        lanes = slice(half * B, half * B + B)
        back_right[half * H : half * H + H, lanes] = twice * c[:H]
        back_right[B + half * H : B + half * H + H, lanes] = imag
    return tuple(np.asarray(t, np.float32).astype(BF16) for t in (right, left, middle, back_left, back_right))


def dot(a, b):
    return jnp.dot(a, b, preferred_element_type=F32)


def shifted(x, off):
    rows = x.shape[0]
    if off == 0:
        return x
    gap = jnp.zeros((rows, abs(off)), x.dtype)
    if off > 0:
        return jnp.concatenate([x[:, off:], gap], 1)
    return jnp.concatenate([gap, x[:, :off]], 1)


def banded(taps_ref, which, valid):
    high, low = [], []
    for b in range(5):
        band = jnp.zeros(which.shape, F32)
        for a in range(5):
            band = jnp.where(which == a, taps_ref[0, 0, 5 * a + b], band)
        if valid is not None:
            band = jnp.where(valid, band, 0.0)
        top = band.astype(BF16)
        high.append(top)
        low.append((band - top.astype(F32)).astype(BF16))
    return jnp.concatenate([jnp.concatenate(high, 1), jnp.concatenate(low, 1)], 0)


def prepare_kernel(image, last, head, sems):
    rows = image.shape[1]
    pairs = ((image.at[0, pl.ds(rows - EDGE, EDGE)], last), (image.at[0, pl.ds(0, EDGE)], head))
    copies = [pltpu.make_async_copy(whence, where, sems.at[n]) for n, (whence, where) in enumerate(pairs)]
    for copy in copies:
        copy.start()
    for copy in copies:
        copy.wait()


def front_kernel(
    taps_ref, src_ref, count_ref, low_ref, high_ref, image_ref, weight_ref, anchor, out, first, blocks_ref, keep_sem, out_sems
):
    keep_first = pltpu.make_async_copy(anchor.at[pl.ds(0, 1)], first, keep_sem)
    keep_first.start()
    x_ref = image_ref.at[0]
    rows, cols = x_ref.shape
    across = cols // B
    count = rows // B * across
    blocks_ref[count] = jnp.zeros((B, B), BF16)
    i = lax.broadcasted_iota(jnp.int32, (rows, rows), 0)
    j = lax.broadcasted_iota(jnp.int32, (rows, rows), 1)
    bands = banded(taps_ref, j - i + 2, None)
    e = lax.broadcasted_iota(jnp.int32, (2 * EDGE, 2 * EDGE), 0)
    k = lax.broadcasted_iota(jnp.int32, (2 * EDGE, 2 * EDGE), 1)
    upper = (e < EDGE) & (k < EDGE)
    lower = (e >= EDGE) & (k >= EDGE)
    which = jnp.where(upper, k - (EDGE - 2) - e, k + (EDGE + 2) - e)
    rim = jnp.concatenate([low_ref[...], high_ref[...]], 0)
    rims = jnp.concatenate([shifted(rim, b - 2) for b in range(5)], 0)
    edge = dot(banded(taps_ref, which, upper | lower), rims)
    edge = edge[: 2 * EDGE] + edge[2 * EDGE :]
    x = x_ref[...]
    stack = jnp.concatenate([shifted(x, b - 2) for b in range(5)], 0)
    both = dot(bands, stack)
    corrected = both[:rows] + both[rows:]
    corrected = jnp.concatenate(
        [corrected[:EDGE] + edge[:EDGE], corrected[EDGE : rows - EDGE], corrected[rows - EDGE :] + edge[EDGE:]], 0
    )
    weighted = (corrected * weight_ref[0].astype(F32)).astype(BF16)
    for k in range(count):
        r, c = k // across * B, k % across * B
        blocks_ref[k] = weighted[r : r + B, c : c + B]
    sends = []
    for d in range(out.shape[0]):
        for q in range(out.shape[1]):
            at = jnp.where(q < count_ref[0, 0, d], src_ref[0, 0, d, q], count)
            sends.append(pltpu.make_async_copy(blocks_ref.at[at], out.at[d, q], out_sems.at[d, q]))
            sends[-1].start()
    keep_first.wait()
    for send in sends:
        send.wait()


def strip_kernel(dst_ref, in_ref, a_ref, b_ref, first_ref, acc_ref):
    acc_ref[...] = jnp.zeros_like(acc_ref)
    for d in range(in_ref.shape[0]):
        for q in range(in_ref.shape[1]):
            j = dst_ref[0, d, 0, q]
            acc_ref[j] = acc_ref[j] + in_ref[d, q].astype(F32)
    a_ref[...] = acc_ref[: HALF + 1].astype(BF16)
    b_ref[: HALF - 1] = acc_ref[HALF + 1 :].astype(BF16)
    b_ref[HALF - 1] = jnp.zeros((B, B), BF16)
    first_ref[0] = acc_ref[0].astype(BF16)


def forward(blocks, right, left, middle):
    pairs = jnp.concatenate([jnp.concatenate([blocks[m], blocks[m + 1]], 1) for m in range(HALF)], 0)
    p = dot(pairs, right).astype(BF16)
    re = [p[m * B : m * B + B, :B] for m in range(HALF)]
    im = [p[m * B : m * B + B, B:] for m in range(HALF)]
    spectra = dot(left, jnp.concatenate([jnp.concatenate(re, 1), jnp.concatenate(im, 1)], 0))
    p = dot(jnp.concatenate(blocks, 1), middle).astype(BF16)
    return spectra, dot(left[:, :B], p)


def current_kernel(a_ref, b_ref, right_ref, left_ref, middle_ref, out_ref):
    blocks = [a_ref[m] for m in range(HALF + 1)] + [b_ref[m] for m in range(HALF)]
    for part in range(2):
        spectra, rest = forward(blocks[part * HALF : part * HALF + HALF + 1], right_ref[...], left_ref[...], middle_ref[...])
        out_ref[part, :, : HALF * B] = spectra.astype(BF16)
        out_ref[part, :, HALF * B :] = rest.astype(BF16)


def correlate_chunk(cur_ref, part, blocks, right, left, middle, back_left, back_right, out_ref, cross_ref, mag_ref):
    lane = lax.broadcasted_iota(jnp.int32, (1, B), 1)
    twice = jnp.where(lane % H == 0, 1.0, 2.0)
    sums = []
    spectra, rest = forward(blocks, right, left, middle)
    for m in range(HALF + 1):
        f = spectra[:, m * B : m * B + B] if m < HALF else rest
        c = cur_ref[part, :, m * B : m * B + B].astype(F32)
        ar, ai, br, bi = c[:B], c[B:], f[:B], f[B:]
        re = ar * br + ai * bi
        im = ai * br - ar * bi
        square = re * re + im * im
        mag = square * lax.rsqrt(jnp.maximum(square, 1e-30))
        cross_ref[m, :B] = re
        cross_ref[m, B:] = im
        mag_ref[m] = mag
        total = jnp.sum(mag, axis=0, keepdims=True)
        sums.append(total * twice if m < HALF else total)
    row = lax.broadcasted_iota(jnp.int32, (HALF, B), 0)
    lanes = lax.broadcasted_iota(jnp.int32, (HALF, B), 1)
    mine = row == lanes % H
    table = jnp.concatenate(sums[:HALF], 0) + jnp.where(mine, sums[HALF], 0.0)
    aligned = lanes < H
    first = jnp.sum(jnp.where(aligned, table, 0.0), axis=1, keepdims=True)
    second = jnp.sum(jnp.where(aligned, 0.0, table), axis=1, keepdims=True)
    floor = jnp.where(aligned, first, second) * (0.1 / (B * B)) + 1e-6
    floor_middle = jnp.sum(jnp.where(mine, floor, 0.0), axis=0, keepdims=True)
    floor_middle = jnp.where(lane % H < HALF, floor_middle, 1.0)

    def whitened(m, low):
        scale = 1.0 / (mag_ref[m] + low)
        return jnp.concatenate([cross_ref[m, :B] * scale, cross_ref[m, B:] * scale], 0).astype(BF16)

    y_middle = dot(back_left[:B], whitened(HALF, floor_middle))
    y = dot(back_left, jnp.concatenate([whitened(m, floor[m : m + 1]) for m in range(HALF)], 1))
    is_zero = lane % H == 0
    both = []
    for m in range(HALF):
        turned = y_middle if m == 0 else pltpu.roll(y_middle, B - m, 1)
        imag = jnp.where(is_zero, turned, y[B:, m * B : m * B + B])
        both.append(jnp.concatenate([y[:B, m * B : m * B + B].astype(BF16), imag.astype(BF16)], 1))
    result = dot(jnp.concatenate(both, 0), back_right)
    for m in range(HALF):
        out_ref[0, 2 * m] = result[m * B : m * B + B, :B]
        out_ref[0, 2 * m + 1] = result[m * B : m * B + B, B:]


def first_half_kernel(cur_ref, a_ref, anchor_ref, right, left, middle, back_left, back_right, out_ref, cross_ref, mag_ref):
    is_first = lax.axis_index("sec") == 0
    blocks = [jnp.where(is_first, anchor_ref[m], a_ref[m]) for m in range(HALF + 1)]
    correlate_chunk(cur_ref, 0, blocks, right[...], left[...], middle[...], back_left[...], back_right[...], out_ref, cross_ref, mag_ref)


def second_half_kernel(
    held_ref, cur_ref, a_ref, b_ref, anchor_ref, border_ref, right, left, middle, back_left, back_right, out_ref, cross_ref, mag_ref
):
    del held_ref
    is_first = lax.axis_index("sec") == 0
    blocks = [jnp.where(is_first, anchor_ref[HALF], a_ref[HALF])]
    blocks += [jnp.where(is_first, anchor_ref[HALF + 1 + m], b_ref[m]) for m in range(HALF - 1)]
    blocks += [jnp.where(is_first, border_ref[0], b_ref[HALF - 1])]
    correlate_chunk(cur_ref, 1, blocks, right[...], left[...], middle[...], back_left[...], back_right[...], out_ref, cross_ref, mag_ref)


SMEM = pl.BlockSpec(memory_space=pltpu.SMEM)
VMEM = pl.BlockSpec(memory_space=pltpu.VMEM)
ANY = pl.BlockSpec(memory_space=pl.ANY)
HBM = pl.BlockSpec(memory_space=pltpu.HBM)


def call(kernel, out_shape, in_specs, out_specs, scratch, flops, moved, args, aliases=None, grid=None, limit=VMEM_LIMIT):
    extra = {} if grid is None else {"grid": grid}
    return pl.pallas_call(
        kernel,
        out_shape=out_shape,
        in_specs=in_specs,
        out_specs=out_specs,
        scratch_shapes=scratch,
        input_output_aliases=aliases or {},
        compiler_params=pltpu.CompilerParams(vmem_limit_bytes=limit),
        cost_estimate=pl.CostEstimate(flops=flops, bytes_accessed=moved, transcendentals=0),
        **extra,
    )(*args)


def body(image, weight, lens_filter_taps, block_src, block_dst, valid_count, anchor):
    rows, cols = image.shape[1:]
    strips = lax.axis_size("tile")
    sections = lax.axis_size("sec")
    slots = block_src.shape[-1]
    count = anchor.shape[0]
    shape = jax.ShapeDtypeStruct
    whole = lambda *dims: pl.BlockSpec(dims, lambda i: (0,) * len(dims))
    forth = [(i, i + 1) for i in range(strips - 1)]
    back = [(i + 1, i) for i in range(strips - 1)]
    last, head = call(
        prepare_kernel,
        (shape((EDGE, cols), BF16), shape((EDGE, cols), BF16)),
        [HBM],
        (VMEM,) * 2,
        [pltpu.SemaphoreType.DMA((2,))],
        2**33,
        2**17,
        (image,),
        limit=PREPARE_VMEM_LIMIT,
    )
    low = lax.ppermute(last, "tile", forth)
    high = lax.ppermute(head, "tile", back)
    tile_blocks = rows // B * (cols // B)
    outgoing, anchor_first = call(
        front_kernel,
        (shape((strips, slots, B, B), BF16), shape((1, B, B), BF16)),
        [SMEM] * 3 + [VMEM] * 4 + [HBM],
        (HBM, HBM),
        [
            pltpu.VMEM((tile_blocks + 1, B, B), BF16),
            pltpu.SemaphoreType.DMA,
            pltpu.SemaphoreType.DMA((strips, slots)),
        ],
        2 * 10 * rows * rows * cols,
        4 * 2 * rows * cols,
        (lens_filter_taps, block_src, valid_count, low, high, image, weight, anchor),
    )
    incoming = lax.all_to_all(outgoing, "tile", split_axis=0, concat_axis=0, tiled=True)
    border = lax.ppermute(anchor_first, "tile", back)
    incoming, border = lax.optimization_barrier((incoming, border))
    part_a, part_b, first = call(
        strip_kernel,
        (shape((HALF + 1, B, B), BF16), shape((HALF, B, B), BF16), shape((1, B, B), BF16)),
        [SMEM, VMEM],
        (VMEM, VMEM, VMEM),
        [pltpu.VMEM((count, B, B), F32)],
        2**20,
        4 * 2 * rows * cols,
        (block_dst, incoming),
    )
    on = [(i, i + 1) for i in range(sections - 1)]
    prior_a = lax.ppermute(part_a, "sec", on)
    own_rim = lax.ppermute(first, "tile", back)
    part_b = lax.dynamic_update_slice(part_b, own_rim, (HALF - 1, 0, 0))
    prior_b = lax.ppermute(part_b, "sec", on)
    right, left, middle, back_left, back_right = (jnp.asarray(t) for t in tables())
    spectra = call(
        current_kernel,
        shape((2, 2 * B, (HALF + 1) * B), BF16),
        [VMEM] * 5,
        VMEM,
        [],
        2 * 16 * count * B**3,
        8 * count * B * B,
        (part_a, part_b, right, left, middle),
    )
    windows = 2 * count
    scratch = [pltpu.VMEM((HALF + 1, 2 * B, B), F32), pltpu.VMEM((HALF + 1, B, B), F32)]
    half = lambda at: pl.BlockSpec((1, windows // 2, B, B), lambda i: (0, at, 0, 0))
    result = shape((1, windows, B, B), F32)
    held = call(
        first_half_kernel,
        result,
        [VMEM] * 8,
        half(0),
        scratch,
        2 * 16 * count * B**3,
        12 * count * B * B,
        (spectra, prior_a, anchor, right, left, middle, back_left, back_right),
        grid=(1,),
    )
    return call(
        second_half_kernel,
        result,
        [ANY] + [VMEM] * 10,
        half(1),
        scratch,
        2 * 16 * count * B**3,
        12 * count * B * B,
        (held, spectra, prior_a, prior_b, anchor, border, right, left, middle, back_left, back_right),
        aliases={0: 0},
        grid=(1,),
    )


def solution(mesh):
    in_specs = (
        P("sec", "tile", None),
        P("sec", "tile", None),
        P("sec", "tile", None),
        P("sec", "tile", None, None),
        P("sec", None, "tile", None),
        P("sec", "tile", None),
        P("tile", None, None),
    )
    out_specs = P("sec", "tile", None, None)
    return jax.shard_map(body, mesh=mesh, in_specs=in_specs, out_specs=out_specs, check_vma=False)
```

```python
import jax
import jax.numpy as jnp
import numpy as np
from jax import lax
from jax.experimental import pallas as pl
from jax.experimental.pallas import tpu as pltpu
from jax.sharding import PartitionSpec as P

B = 128
H = B // 2
EDGE = 16
EARLY = 8
PAIRS = 9
F32 = jnp.float32
BF16 = jnp.bfloat16
VMEM_LIMIT = 48 * 2**20
PREPARE_VMEM_LIMIT = 54912 * 2**10


def tables():
    j = np.arange(B)
    angle = (j[:, None] * j[None, :] % B) * (2.0 * np.pi / B)
    c, s = np.cos(angle), np.sin(angle)
    right = np.zeros((2 * B, 2 * B))
    for half, start in ((0, 0), (1, H)):
        right[start : start + B, half * H : half * H + H] = c[:, :H]
        right[start : start + B, B + half * H : B + half * H + H] = s[:, :H]
    left = np.block([[c, -s], [-s, -c]])
    q = np.arange((PAIRS + 1) * B)
    sign = 1.0 - 2.0 * (q % 2)
    middle = np.zeros(((PAIRS + 1) * B, B))
    for m in range(PAIRS):
        middle[:, m] = sign * (q // B == m)
        middle[:, H + m] = sign * ((q - H) // B == m)
    back_left = np.block([[c, -s], [s, c]])
    twice = np.where(j[:H] == 0, 1.0, 2.0)[:, None] / B
    back_right = np.zeros((2 * B, 2 * B))
    imag = -twice * s[:H]
    imag[0] = (1.0 - 2.0 * (j % 2)) / B
    for half in range(2):
        lanes = slice(half * B, half * B + B)
        back_right[half * H : half * H + H, lanes] = twice * c[:H]
        back_right[B + half * H : B + half * H + H, lanes] = imag
    return tuple(np.asarray(t, np.float32).astype(BF16) for t in (right, left, middle, back_left, back_right))


def dot(a, b):
    return jnp.dot(a, b, preferred_element_type=F32)


def shifted(x, off):
    rows = x.shape[0]
    if off == 0:
        return x
    gap = jnp.zeros((rows, abs(off)), x.dtype)
    if off > 0:
        return jnp.concatenate([x[:, off:], gap], 1)
    return jnp.concatenate([gap, x[:, :off]], 1)


def banded(taps_ref, which, valid):
    high, low = [], []
    for b in range(5):
        band = jnp.zeros(which.shape, F32)
        for a in range(5):
            band = jnp.where(which == a, taps_ref[0, 0, 5 * a + b], band)
        if valid is not None:
            band = jnp.where(valid, band, 0.0)
        top = band.astype(BF16)
        high.append(top)
        low.append((band - top.astype(F32)).astype(BF16))
    return jnp.concatenate([jnp.concatenate(high, 1), jnp.concatenate(low, 1)], 0)


def prepare_kernel(image, last, head, sems):
    rows = image.shape[1]
    pairs = ((image.at[0, pl.ds(rows - EDGE, EDGE)], last), (image.at[0, pl.ds(0, EDGE)], head))
    copies = [pltpu.make_async_copy(whence, where, sems.at[n]) for n, (whence, where) in enumerate(pairs)]
    for copy in copies:
        copy.start()
    for copy in copies:
        copy.wait()


def lens_kernel(taps_ref, image_ref, weight_ref, blocks_ref, edge_ref):
    x = image_ref[0]
    rows, cols = x.shape
    across = cols // B
    i = lax.broadcasted_iota(jnp.int32, (rows, rows), 0)
    j = lax.broadcasted_iota(jnp.int32, (rows, rows), 1)
    bands = banded(taps_ref, j - i + 2, None)
    stack = jnp.concatenate([shifted(x, b - 2) for b in range(5)], 0)
    both = dot(bands, stack)
    corrected = both[:rows] + both[rows:]
    edge_ref[:EDGE] = corrected[:EDGE]
    edge_ref[EDGE:] = corrected[rows - EDGE :]
    weighted = (corrected * weight_ref[0].astype(F32)).astype(BF16)
    for k in range(rows // B * across):
        r, c = k // across * B, k % across * B
        blocks_ref[k] = weighted[r : r + B, c : c + B]


def pick_kernel(
    taps_ref, src_ref, count_ref, low_ref, high_ref, edge_ref, weight_ref, blocks_ref, anchor_ref, out, first_ref, fixed_ref, out_sems
):
    rows, cols = weight_ref.shape[1:]
    across = cols // B
    count = rows // B * across
    for k in range(count):
        fixed_ref[k] = blocks_ref[k]
    fixed_ref[count] = jnp.zeros((B, B), BF16)
    first_ref[0] = anchor_ref[0]
    e = lax.broadcasted_iota(jnp.int32, (2 * EDGE, 2 * EDGE), 0)
    k = lax.broadcasted_iota(jnp.int32, (2 * EDGE, 2 * EDGE), 1)
    upper = (e < EDGE) & (k < EDGE)
    lower = (e >= EDGE) & (k >= EDGE)
    which = jnp.where(upper, k - (EDGE - 2) - e, k + (EDGE + 2) - e)
    rim = jnp.concatenate([low_ref[...], high_ref[...]], 0)
    rims = jnp.concatenate([shifted(rim, b - 2) for b in range(5)], 0)
    both = dot(banded(taps_ref, which, upper | lower), rims)
    corrected = edge_ref[...] + (both[: 2 * EDGE] + both[2 * EDGE :])
    top = (corrected[:EDGE] * weight_ref[0, :EDGE].astype(F32)).astype(BF16)
    bottom = (corrected[EDGE:] * weight_ref[0, rows - EDGE :].astype(F32)).astype(BF16)
    for c in range(across):
        fixed_ref[c, :EDGE] = top[:, c * B : c * B + B]
        fixed_ref[count - across + c, B - EDGE :] = bottom[:, c * B : c * B + B]
    sends = []
    for d in range(out.shape[0]):
        for q in range(out.shape[1]):
            at = jnp.where(q < count_ref[0, 0, d], src_ref[0, 0, d, q], count)
            sends.append(pltpu.make_async_copy(fixed_ref.at[at], out.at[d, q], out_sems.at[d, q]))
            sends[-1].start()
    for send in sends:
        send.wait()


def strip_kernel(dst_ref, in_ref, a_ref, rest_ref, acc_ref):
    acc_ref[...] = jnp.zeros_like(acc_ref)
    for d in range(in_ref.shape[0]):
        for q in range(in_ref.shape[1]):
            j = dst_ref[0, d, 0, q]
            acc_ref[j] = acc_ref[j] + in_ref[d, q].astype(F32)
    a_ref[...] = acc_ref[:EARLY].astype(BF16)
    rest_ref[...] = acc_ref[EARLY:]


def rest_kernel(a_ref, rest_ref, b_ref, first_ref):
    count = rest_ref.shape[0]
    b_ref[:count] = rest_ref[...].astype(BF16)
    b_ref[count] = jnp.zeros((B, B), BF16)
    first_ref[0] = a_ref[0]


def forward(blocks, right, left, middle):
    pairs = len(blocks) - 1
    both = jnp.concatenate([jnp.concatenate([blocks[m], blocks[m + 1]], 1) for m in range(pairs)], 0)
    p = dot(both, right).astype(BF16)
    re = [p[m * B : m * B + B, :B] for m in range(pairs)]
    im = [p[m * B : m * B + B, B:] for m in range(pairs)]
    spectra = dot(left, jnp.concatenate([jnp.concatenate(re, 1), jnp.concatenate(im, 1)], 0))
    p = dot(jnp.concatenate(blocks, 1), middle[: (pairs + 1) * B]).astype(BF16)
    return spectra, dot(left[:, :B], p)


def spectra_out(blocks, right_ref, left_ref, middle_ref, out_ref):
    spectra, rest = forward(blocks, right_ref[...], left_ref[...], middle_ref[...])
    out_ref[:, : spectra.shape[1]] = spectra.astype(BF16)
    out_ref[:, spectra.shape[1] :] = rest.astype(BF16)


def early_kernel(a_ref, *refs):
    spectra_out([a_ref[m] for m in range(EARLY)], *refs)


def late_kernel(a_ref, b_ref, *refs):
    spectra_out([a_ref[EARLY - 1]] + [b_ref[m] for m in range(b_ref.shape[0])], *refs)


def correlate_chunk(cur_ref, blocks, tables, out, at, cross_ref, mag_ref, result_ref, sems):
    right, left, middle, back_left, back_right = (table[...] for table in tables)
    pairs = len(blocks) - 1
    lane = lax.broadcasted_iota(jnp.int32, (1, B), 1)
    twice = jnp.where(lane % H == 0, 1.0, 2.0)
    sums = []
    spectra, rest = forward(blocks, right, left, middle)
    for m in range(pairs + 1):
        f = spectra[:, m * B : m * B + B] if m < pairs else rest
        c = cur_ref[:, m * B : m * B + B].astype(F32)
        ar, ai, br, bi = c[:B], c[B:], f[:B], f[B:]
        re = ar * br + ai * bi
        im = ai * br - ar * bi
        square = re * re + im * im
        mag = square * lax.rsqrt(jnp.maximum(square, 1e-30))
        cross_ref[m, :B] = re
        cross_ref[m, B:] = im
        mag_ref[m] = mag
        total = jnp.sum(mag, axis=0, keepdims=True)
        sums.append(total * twice if m < pairs else total)
    row = lax.broadcasted_iota(jnp.int32, (pairs, B), 0)
    lanes = lax.broadcasted_iota(jnp.int32, (pairs, B), 1)
    mine = row == lanes % H
    table = jnp.concatenate(sums[:pairs], 0) + jnp.where(mine, sums[pairs], 0.0)
    aligned = lanes < H
    first = jnp.sum(jnp.where(aligned, table, 0.0), axis=1, keepdims=True)
    second = jnp.sum(jnp.where(aligned, 0.0, table), axis=1, keepdims=True)
    floor = jnp.where(aligned, first, second) * (0.1 / (B * B)) + 1e-6
    floor_middle = jnp.sum(jnp.where(mine, floor, 0.0), axis=0, keepdims=True)
    floor_middle = jnp.where(lane % H < pairs, floor_middle, 1.0)

    def whitened(m, low):
        scale = 1.0 / (mag_ref[m] + low)
        return jnp.concatenate([cross_ref[m, :B] * scale, cross_ref[m, B:] * scale], 0).astype(BF16)

    y_middle = dot(back_left[:B], whitened(pairs, floor_middle))
    y = dot(back_left, jnp.concatenate([whitened(m, floor[m : m + 1]) for m in range(pairs)], 1))
    is_zero = lane % H == 0
    both = []
    for m in range(pairs):
        turned = y_middle if m == 0 else pltpu.roll(y_middle, B - m, 1)
        imag = jnp.where(is_zero, turned, y[B:, m * B : m * B + B])
        both.append(jnp.concatenate([y[:B, m * B : m * B + B].astype(BF16), imag.astype(BF16)], 1))
    result = dot(jnp.concatenate(both, 0), back_right)
    sends = []
    for m in range(pairs):
        result_ref[2 * m] = result[m * B : m * B + B, :B]
        result_ref[2 * m + 1] = result[m * B : m * B + B, B:]
        sends.append(
            pltpu.make_async_copy(result_ref.at[pl.ds(2 * m, 2)], out.at[0, pl.ds(2 * (at + m), 2)], sems.at[m])
        )
        sends[-1].start()
    for send in sends:
        send.wait()


def prior_block(anchor, direct, relayed):
    sec = lax.axis_index("sec")
    chosen = jnp.where(sec == lax.axis_size("sec") // 2, relayed, direct)
    return jnp.where(sec == 0, anchor, chosen)


def correlate_early(cur_ref, a_ref, relay_ref, anchor_ref, *refs):
    blocks = [prior_block(anchor_ref[m], a_ref[m], relay_ref[m]) for m in range(EARLY)]
    correlate_chunk(cur_ref, blocks, refs[:5], refs[5], 0, *refs[6:])


def correlate_late(held, cur_ref, a_ref, relay_ref, b_ref, anchor_ref, border_ref, *refs):
    del held
    is_first = lax.axis_index("sec") == 0
    rest = b_ref.shape[0] - 1
    blocks = [prior_block(anchor_ref[EARLY - 1], a_ref[EARLY - 1], relay_ref[EARLY - 1])]
    blocks += [jnp.where(is_first, anchor_ref[EARLY + m], b_ref[m]) for m in range(rest)]
    blocks += [jnp.where(is_first, border_ref[0], b_ref[rest])]
    correlate_chunk(cur_ref, blocks, refs[:5], refs[5], EARLY - 1, *refs[6:])


SMEM = pl.BlockSpec(memory_space=pltpu.SMEM)
VMEM = pl.BlockSpec(memory_space=pltpu.VMEM)
ANY = pl.BlockSpec(memory_space=pl.ANY)
HBM = pl.BlockSpec(memory_space=pltpu.HBM)


def call(kernel, out_shape, in_specs, out_specs, scratch, flops, moved, args, aliases=None, grid=None, limit=VMEM_LIMIT):
    extra = {} if grid is None else {"grid": grid}
    return pl.pallas_call(
        kernel,
        out_shape=out_shape,
        in_specs=in_specs,
        out_specs=out_specs,
        scratch_shapes=scratch,
        input_output_aliases=aliases or {},
        compiler_params=pltpu.CompilerParams(vmem_limit_bytes=limit),
        cost_estimate=pl.CostEstimate(flops=flops, bytes_accessed=moved, transcendentals=0),
        **extra,
    )(*args)


def body(image, weight, lens_filter_taps, block_src, block_dst, valid_count, anchor):
    rows, cols = image.shape[1:]
    strips = lax.axis_size("tile")
    sections = lax.axis_size("sec")
    slots = block_src.shape[-1]
    count = anchor.shape[0]
    shape = jax.ShapeDtypeStruct
    whole = lambda *dims: pl.BlockSpec(dims, lambda i: (0,) * len(dims))
    forth = [(i, i + 1) for i in range(strips - 1)]
    back = [(i + 1, i) for i in range(strips - 1)]
    last, head = call(
        prepare_kernel,
        (shape((EDGE, cols), BF16), shape((EDGE, cols), BF16)),
        [HBM],
        (VMEM,) * 2,
        [pltpu.SemaphoreType.DMA((2,))],
        2**33,
        2**17,
        (image,),
        limit=PREPARE_VMEM_LIMIT,
    )
    low = lax.ppermute(last, "tile", forth)
    high = lax.ppermute(head, "tile", back)
    tile_blocks = rows // B * (cols // B)
    blocks, edge = call(
        lens_kernel,
        (shape((tile_blocks, B, B), BF16), shape((2 * EDGE, cols), F32)),
        [SMEM, VMEM, VMEM],
        (VMEM, VMEM),
        [],
        2 * 10 * rows * rows * cols,
        3 * 2 * rows * cols,
        (lens_filter_taps, image, weight),
    )
    outgoing, anchor_first = call(
        pick_kernel,
        (shape((strips, slots, B, B), BF16), shape((1, B, B), BF16)),
        [SMEM] * 3 + [VMEM] * 6,
        (HBM, VMEM),
        [pltpu.VMEM((tile_blocks + 1, B, B), BF16), pltpu.SemaphoreType.DMA((strips, slots))],
        2**20,
        4 * 2 * rows * cols,
        (lens_filter_taps, block_src, valid_count, low, high, edge, weight, blocks, anchor),
    )
    incoming = lax.all_to_all(outgoing, "tile", split_axis=0, concat_axis=0, tiled=True)
    border = lax.ppermute(anchor_first, "tile", back)
    incoming, border = lax.optimization_barrier((incoming, border))
    part_a, rest = call(
        strip_kernel,
        (shape((EARLY, B, B), BF16), shape((count - EARLY, B, B), F32)),
        [SMEM, VMEM],
        (VMEM, VMEM),
        [pltpu.VMEM((count, B, B), F32)],
        2**20,
        4 * 2 * rows * cols,
        (block_dst, incoming),
    )
    part_b, first = call(
        rest_kernel,
        (shape((count - EARLY + 1, B, B), BF16), shape((1, B, B), BF16)),
        [VMEM] * 2,
        (VMEM, VMEM),
        [],
        2**18,
        6 * EARLY * B * B,
        (part_a, rest),
    )
    turn, side = sections // 2, strips // 2
    by_relay, forward_on = [], []
    for s in range(sections - 1):
        for d in range(strips):
            here, there = s * strips + d, (s + 1) * strips + d
            if s + 1 == turn:
                relay = there + side if d < side else d - side
                by_relay.append((here, relay))
                forward_on.append((relay, there))
            else:
                by_relay.append((here, there))
    on = [(i, i + 1) for i in range(sections - 1)]
    prior_a = lax.ppermute(part_a, ("sec", "tile"), by_relay)
    own_rim = lax.ppermute(first, "tile", back)
    part_b = lax.dynamic_update_slice(part_b, own_rim, (count - EARLY, 0, 0))
    prior_b = lax.ppermute(part_b, "sec", on)
    right, left, middle, back_left, back_right = (jnp.asarray(t) for t in tables())
    early, late = EARLY - 1, count - EARLY + 1
    current = lambda kernel, pairs, *parts: call(
        kernel,
        shape((2 * B, (pairs + 1) * B), BF16),
        [VMEM] * (len(parts) + 3),
        VMEM,
        [],
        2**10,
        2**10,
        (*parts, right, left, middle),
    )
    spectra_a = current(early_kernel, early, part_a)
    spectra_b = current(late_kernel, late, part_a, part_b)
    prior_a, spectra_b = lax.optimization_barrier((prior_a, spectra_b))
    relayed_a = lax.ppermute(prior_a, ("sec", "tile"), forward_on)
    result = shape((1, 2 * count, B, B), F32)
    scratch = lambda pairs: [
        pltpu.VMEM((pairs + 1, 2 * B, B), F32),
        pltpu.VMEM((pairs + 1, B, B), F32),
        pltpu.VMEM((2 * pairs, B, B), F32),
        pltpu.SemaphoreType.DMA((pairs,)),
    ]
    held = call(
        correlate_early,
        result,
        [VMEM] * 9,
        HBM,
        scratch(early),
        2**10,
        2**10,
        (spectra_a, prior_a, relayed_a, anchor, right, left, middle, back_left, back_right),
    )
    return call(
        correlate_late,
        result,
        [HBM] + [VMEM] * 11,
        HBM,
        scratch(late),
        2**30,
        2**22,
        (held, spectra_b, prior_a, relayed_a, prior_b, anchor, border, right, left, middle, back_left, back_right),
        aliases={0: 0},
    )


def solution(mesh):
    in_specs = (
        P("sec", "tile", None),
        P("sec", "tile", None),
        P("sec", "tile", None),
        P("sec", "tile", None, None),
        P("sec", None, "tile", None),
        P("sec", "tile", None),
        P("tile", None, None),
    )
    out_specs = P("sec", "tile", None, None)
    return jax.shard_map(body, mesh=mesh, in_specs=in_specs, out_specs=out_specs, check_vma=False)
```

```python
import jax
import jax.numpy as jnp
import numpy as np
from jax import lax
from jax.experimental import pallas as pl
from jax.experimental.pallas import tpu as pltpu
from jax.sharding import PartitionSpec as P

B = 128
H = B // 2
EDGE = 16
EARLY = 11
PAIRS = 10
F32 = jnp.float32
BF16 = jnp.bfloat16
VMEM_LIMIT = 48 * 2**20
PREPARE_VMEM_LIMIT = 54912 * 2**10


def tables():
    j = np.arange(B)
    angle = (j[:, None] * j[None, :] % B) * (2.0 * np.pi / B)
    c, s = np.cos(angle), np.sin(angle)
    right = np.zeros((2 * B, 2 * B))
    for half, start in ((0, 0), (1, H)):
        right[start : start + B, half * H : half * H + H] = c[:, :H]
        right[start : start + B, B + half * H : B + half * H + H] = s[:, :H]
    left = np.block([[c, -s], [-s, -c]])
    q = np.arange((PAIRS + 1) * B)
    sign = 1.0 - 2.0 * (q % 2)
    middle = np.zeros(((PAIRS + 1) * B, B))
    for m in range(PAIRS):
        middle[:, m] = sign * (q // B == m)
        middle[:, H + m] = sign * ((q - H) // B == m)
    back_left = np.block([[c, -s], [s, c]])
    twice = np.where(j[:H] == 0, 1.0, 2.0)[:, None] / B
    back_right = np.zeros((2 * B, 2 * B))
    imag = -twice * s[:H]
    imag[0] = (1.0 - 2.0 * (j % 2)) / B
    for half in range(2):
        lanes = slice(half * B, half * B + B)
        back_right[half * H : half * H + H, lanes] = twice * c[:H]
        back_right[B + half * H : B + half * H + H, lanes] = imag
    return tuple(np.asarray(t, np.float32).astype(BF16) for t in (right, left, middle, back_left, back_right))


def dot(a, b):
    return jnp.dot(a, b, preferred_element_type=F32)


def shifted(x, off):
    rows = x.shape[0]
    if off == 0:
        return x
    gap = jnp.zeros((rows, abs(off)), x.dtype)
    if off > 0:
        return jnp.concatenate([x[:, off:], gap], 1)
    return jnp.concatenate([gap, x[:, :off]], 1)


def banded(taps_ref, which, valid):
    high, low = [], []
    for b in range(5):
        band = jnp.zeros(which.shape, F32)
        for a in range(5):
            band = jnp.where(which == a, taps_ref[0, 0, 5 * a + b], band)
        if valid is not None:
            band = jnp.where(valid, band, 0.0)
        top = band.astype(BF16)
        high.append(top)
        low.append((band - top.astype(F32)).astype(BF16))
    return jnp.concatenate([jnp.concatenate(high, 1), jnp.concatenate(low, 1)], 0)


def prepare_kernel(image, last, head, sems):
    rows = image.shape[1]
    pairs = ((image.at[0, pl.ds(rows - EDGE, EDGE)], last), (image.at[0, pl.ds(0, EDGE)], head))
    copies = [pltpu.make_async_copy(whence, where, sems.at[n]) for n, (whence, where) in enumerate(pairs)]
    for copy in copies:
        copy.start()
    for copy in copies:
        copy.wait()


def lens_kernel(taps_ref, image_ref, weight_ref, blocks_ref, edge_ref):
    x = image_ref[0]
    rows, cols = x.shape
    across = cols // B
    i = lax.broadcasted_iota(jnp.int32, (rows, rows), 0)
    j = lax.broadcasted_iota(jnp.int32, (rows, rows), 1)
    bands = banded(taps_ref, j - i + 2, None)
    stack = jnp.concatenate([shifted(x, b - 2) for b in range(5)], 0)
    both = dot(bands, stack)
    corrected = both[:rows] + both[rows:]
    edge_ref[:EDGE] = corrected[:EDGE]
    edge_ref[EDGE:] = corrected[rows - EDGE :]
    weighted = (corrected * weight_ref[0].astype(F32)).astype(BF16)
    for k in range(rows // B * across):
        r, c = k // across * B, k % across * B
        blocks_ref[k] = weighted[r : r + B, c : c + B]


def pick_kernel(
    taps_ref, src_ref, count_ref, low_ref, high_ref, edge_ref, weight_ref, blocks_ref, anchor_ref, out, first_ref, fixed_ref, out_sems
):
    rows, cols = weight_ref.shape[1:]
    across = cols // B
    count = rows // B * across
    for k in range(count):
        fixed_ref[k] = blocks_ref[k]
    fixed_ref[count] = jnp.zeros((B, B), BF16)
    first_ref[0] = anchor_ref[0]
    e = lax.broadcasted_iota(jnp.int32, (2 * EDGE, 2 * EDGE), 0)
    k = lax.broadcasted_iota(jnp.int32, (2 * EDGE, 2 * EDGE), 1)
    upper = (e < EDGE) & (k < EDGE)
    lower = (e >= EDGE) & (k >= EDGE)
    which = jnp.where(upper, k - (EDGE - 2) - e, k + (EDGE + 2) - e)
    rim = jnp.concatenate([low_ref[...], high_ref[...]], 0)
    rims = jnp.concatenate([shifted(rim, b - 2) for b in range(5)], 0)
    both = dot(banded(taps_ref, which, upper | lower), rims)
    corrected = edge_ref[...] + (both[: 2 * EDGE] + both[2 * EDGE :])
    top = (corrected[:EDGE] * weight_ref[0, :EDGE].astype(F32)).astype(BF16)
    bottom = (corrected[EDGE:] * weight_ref[0, rows - EDGE :].astype(F32)).astype(BF16)
    for c in range(across):
        fixed_ref[c, :EDGE] = top[:, c * B : c * B + B]
        fixed_ref[count - across + c, B - EDGE :] = bottom[:, c * B : c * B + B]
    sends = []
    for d in range(out.shape[0]):
        for q in range(out.shape[1]):
            at = jnp.where(q < count_ref[0, 0, d], src_ref[0, 0, d, q], count)
            sends.append(pltpu.make_async_copy(fixed_ref.at[at], out.at[d, q], out_sems.at[d, q]))
            sends[-1].start()
    for send in sends:
        send.wait()


def strip_kernel(dst_ref, in_ref, a_ref, rest_ref, acc_ref):
    acc_ref[...] = jnp.zeros_like(acc_ref)
    for d in range(in_ref.shape[0]):
        for q in range(in_ref.shape[1]):
            j = dst_ref[0, d, 0, q]
            acc_ref[j] = acc_ref[j] + in_ref[d, q].astype(F32)
    a_ref[...] = acc_ref[:EARLY].astype(BF16)
    rest_ref[...] = acc_ref[EARLY:]


def rest_kernel(a_ref, rest_ref, b_ref, first_ref):
    count = rest_ref.shape[0]
    b_ref[:count] = rest_ref[...].astype(BF16)
    b_ref[count] = jnp.zeros((B, B), BF16)
    first_ref[0] = a_ref[0]


def forward(blocks, right, left, middle):
    pairs = len(blocks) - 1
    both = jnp.concatenate([jnp.concatenate([blocks[m], blocks[m + 1]], 1) for m in range(pairs)], 0)
    p = dot(both, right).astype(BF16)
    re = [p[m * B : m * B + B, :B] for m in range(pairs)]
    im = [p[m * B : m * B + B, B:] for m in range(pairs)]
    spectra = dot(left, jnp.concatenate([jnp.concatenate(re, 1), jnp.concatenate(im, 1)], 0))
    p = dot(jnp.concatenate(blocks, 1), middle[: (pairs + 1) * B]).astype(BF16)
    return spectra, dot(left[:, :B], p)


def spectra_out(blocks, right_ref, left_ref, middle_ref, out_ref):
    spectra, rest = forward(blocks, right_ref[...], left_ref[...], middle_ref[...])
    out_ref[:, : spectra.shape[1]] = spectra.astype(BF16)
    out_ref[:, spectra.shape[1] :] = rest.astype(BF16)


def early_kernel(a_ref, *refs):
    spectra_out([a_ref[m] for m in range(EARLY)], *refs)


def late_kernel(a_ref, b_ref, *refs):
    spectra_out([a_ref[EARLY - 1]] + [b_ref[m] for m in range(b_ref.shape[0])], *refs)


def correlate_chunk(cur_ref, blocks, tables, out, at, cross_ref, mag_ref, result_ref, sems):
    right, left, middle, back_left, back_right = (table[...] for table in tables)
    pairs = len(blocks) - 1
    lane = lax.broadcasted_iota(jnp.int32, (1, B), 1)
    twice = jnp.where(lane % H == 0, 1.0, 2.0)
    sums = []
    spectra, rest = forward(blocks, right, left, middle)
    for m in range(pairs + 1):
        f = spectra[:, m * B : m * B + B] if m < pairs else rest
        c = cur_ref[:, m * B : m * B + B].astype(F32)
        ar, ai, br, bi = c[:B], c[B:], f[:B], f[B:]
        re = ar * br + ai * bi
        im = ai * br - ar * bi
        square = re * re + im * im
        mag = square * lax.rsqrt(jnp.maximum(square, 1e-30))
        cross_ref[m, :B] = re
        cross_ref[m, B:] = im
        mag_ref[m] = mag
        total = jnp.sum(mag, axis=0, keepdims=True)
        sums.append(total * twice if m < pairs else total)
    row = lax.broadcasted_iota(jnp.int32, (pairs, B), 0)
    lanes = lax.broadcasted_iota(jnp.int32, (pairs, B), 1)
    mine = row == lanes % H
    table = jnp.concatenate(sums[:pairs], 0) + jnp.where(mine, sums[pairs], 0.0)
    aligned = lanes < H
    first = jnp.sum(jnp.where(aligned, table, 0.0), axis=1, keepdims=True)
    second = jnp.sum(jnp.where(aligned, 0.0, table), axis=1, keepdims=True)
    floor = jnp.where(aligned, first, second) * (0.1 / (B * B)) + 1e-6
    floor_middle = jnp.sum(jnp.where(mine, floor, 0.0), axis=0, keepdims=True)
    floor_middle = jnp.where(lane % H < pairs, floor_middle, 1.0)

    def whitened(m, low):
        scale = 1.0 / (mag_ref[m] + low)
        return jnp.concatenate([cross_ref[m, :B] * scale, cross_ref[m, B:] * scale], 0).astype(BF16)

    y_middle = dot(back_left[:B], whitened(pairs, floor_middle))
    y = dot(back_left, jnp.concatenate([whitened(m, floor[m : m + 1]) for m in range(pairs)], 1))
    is_zero = lane % H == 0
    both = []
    for m in range(pairs):
        turned = y_middle if m == 0 else pltpu.roll(y_middle, B - m, 1)
        imag = jnp.where(is_zero, turned, y[B:, m * B : m * B + B])
        both.append(jnp.concatenate([y[:B, m * B : m * B + B].astype(BF16), imag.astype(BF16)], 1))
    result = dot(jnp.concatenate(both, 0), back_right)
    sends = []
    for m in range(pairs):
        result_ref[2 * m] = result[m * B : m * B + B, :B]
        result_ref[2 * m + 1] = result[m * B : m * B + B, B:]
        sends.append(
            pltpu.make_async_copy(result_ref.at[pl.ds(2 * m, 2)], out.at[0, pl.ds(2 * (at + m), 2)], sems.at[m])
        )
        sends[-1].start()
    for send in sends:
        send.wait()


def correlate_early(cur_ref, a_ref, anchor_ref, *refs):
    is_first = lax.axis_index("sec") == 0
    blocks = [jnp.where(is_first, anchor_ref[m], a_ref[m]) for m in range(EARLY)]
    correlate_chunk(cur_ref, blocks, refs[:5], refs[5], 0, *refs[6:])


def correlate_late(held, cur_ref, a_ref, b_ref, anchor_ref, border_ref, *refs):
    del held
    is_first = lax.axis_index("sec") == 0
    rest = b_ref.shape[0] - 1
    blocks = [jnp.where(is_first, anchor_ref[EARLY - 1], a_ref[EARLY - 1])]
    blocks += [jnp.where(is_first, anchor_ref[EARLY + m], b_ref[m]) for m in range(rest)]
    blocks += [jnp.where(is_first, border_ref[0], b_ref[rest])]
    correlate_chunk(cur_ref, blocks, refs[:5], refs[5], EARLY - 1, *refs[6:])


SMEM = pl.BlockSpec(memory_space=pltpu.SMEM)
VMEM = pl.BlockSpec(memory_space=pltpu.VMEM)
ANY = pl.BlockSpec(memory_space=pl.ANY)
HBM = pl.BlockSpec(memory_space=pltpu.HBM)


def call(kernel, out_shape, in_specs, out_specs, scratch, flops, moved, args, aliases=None, grid=None, limit=VMEM_LIMIT):
    extra = {} if grid is None else {"grid": grid}
    return pl.pallas_call(
        kernel,
        out_shape=out_shape,
        in_specs=in_specs,
        out_specs=out_specs,
        scratch_shapes=scratch,
        input_output_aliases=aliases or {},
        compiler_params=pltpu.CompilerParams(vmem_limit_bytes=limit),
        cost_estimate=pl.CostEstimate(flops=flops, bytes_accessed=moved, transcendentals=0),
        **extra,
    )(*args)


def body(image, weight, lens_filter_taps, block_src, block_dst, valid_count, anchor):
    rows, cols = image.shape[1:]
    strips = lax.axis_size("tile")
    sections = lax.axis_size("sec")
    slots = block_src.shape[-1]
    count = anchor.shape[0]
    shape = jax.ShapeDtypeStruct
    whole = lambda *dims: pl.BlockSpec(dims, lambda i: (0,) * len(dims))
    forth = [(i, i + 1) for i in range(strips - 1)]
    back = [(i + 1, i) for i in range(strips - 1)]
    last, head = call(
        prepare_kernel,
        (shape((EDGE, cols), BF16), shape((EDGE, cols), BF16)),
        [HBM],
        (VMEM,) * 2,
        [pltpu.SemaphoreType.DMA((2,))],
        2**33,
        2**17,
        (image,),
        limit=PREPARE_VMEM_LIMIT,
    )
    low = lax.ppermute(last, "tile", forth)
    high = lax.ppermute(head, "tile", back)
    tile_blocks = rows // B * (cols // B)
    blocks, edge = call(
        lens_kernel,
        (shape((tile_blocks, B, B), BF16), shape((2 * EDGE, cols), F32)),
        [SMEM, VMEM, VMEM],
        (VMEM, VMEM),
        [],
        2 * 10 * rows * rows * cols,
        3 * 2 * rows * cols,
        (lens_filter_taps, image, weight),
    )
    outgoing, anchor_first = call(
        pick_kernel,
        (shape((strips, slots, B, B), BF16), shape((1, B, B), BF16)),
        [SMEM] * 3 + [VMEM] * 6,
        (HBM, VMEM),
        [pltpu.VMEM((tile_blocks + 1, B, B), BF16), pltpu.SemaphoreType.DMA((strips, slots))],
        2**20,
        4 * 2 * rows * cols,
        (lens_filter_taps, block_src, valid_count, low, high, edge, weight, blocks, anchor),
    )
    incoming = lax.all_to_all(outgoing, "tile", split_axis=0, concat_axis=0, tiled=True)
    border = lax.ppermute(anchor_first, "tile", back)
    incoming, border = lax.optimization_barrier((incoming, border))
    part_a, rest = call(
        strip_kernel,
        (shape((EARLY, B, B), BF16), shape((count - EARLY, B, B), F32)),
        [SMEM, VMEM],
        (VMEM, VMEM),
        [pltpu.VMEM((count, B, B), F32)],
        2**20,
        4 * 2 * rows * cols,
        (block_dst, incoming),
    )
    part_b, first = call(
        rest_kernel,
        (shape((count - EARLY + 1, B, B), BF16), shape((1, B, B), BF16)),
        [VMEM] * 2,
        (VMEM, VMEM),
        [],
        2**18,
        6 * EARLY * B * B,
        (part_a, rest),
    )
    on = [(i, i + 1) for i in range(sections - 1)]
    prior_a = lax.ppermute(part_a, "sec", on)
    own_rim = lax.ppermute(first, "tile", back)
    part_b = lax.dynamic_update_slice(part_b, own_rim, (count - EARLY, 0, 0))
    prior_b = lax.ppermute(part_b, "sec", on)
    right, left, middle, back_left, back_right = (jnp.asarray(t) for t in tables())
    early, late = EARLY - 1, count - EARLY + 1
    current = lambda kernel, pairs, *parts: call(
        kernel,
        shape((2 * B, (pairs + 1) * B), BF16),
        [VMEM] * (len(parts) + 3),
        VMEM,
        [],
        2**10,
        2**10,
        (*parts, right, left, middle),
    )
    spectra_a = current(early_kernel, early, part_a)
    spectra_b = current(late_kernel, late, part_a, part_b)
    result = shape((1, 2 * count, B, B), F32)
    scratch = lambda pairs: [
        pltpu.VMEM((pairs + 1, 2 * B, B), F32),
        pltpu.VMEM((pairs + 1, B, B), F32),
        pltpu.VMEM((2 * pairs, B, B), F32),
        pltpu.SemaphoreType.DMA((pairs,)),
    ]
    held = call(
        correlate_early,
        result,
        [VMEM] * 8,
        HBM,
        scratch(early),
        2**10,
        2**10,
        (spectra_a, prior_a, anchor, right, left, middle, back_left, back_right),
    )
    return call(
        correlate_late,
        result,
        [HBM] + [VMEM] * 10,
        HBM,
        scratch(late),
        2**30,
        2**22,
        (held, spectra_b, prior_a, prior_b, anchor, border, right, left, middle, back_left, back_right),
        aliases={0: 0},
    )


def solution(mesh):
    in_specs = (
        P("sec", "tile", None),
        P("sec", "tile", None),
        P("sec", "tile", None),
        P("sec", "tile", None, None),
        P("sec", None, "tile", None),
        P("sec", "tile", None),
        P("tile", None, None),
    )
    out_specs = P("sec", "tile", None, None)
    return jax.shard_map(body, mesh=mesh, in_specs=in_specs, out_specs=out_specs, check_vma=False)
```

```python
import jax
import jax.numpy as jnp
import numpy as np
from jax import lax
from jax.experimental import pallas as pl
from jax.experimental.pallas import tpu as pltpu
from jax.sharding import PartitionSpec as P

B = 128
H = B // 2
EDGE = 16
EARLY = 11
PAIRS = 10
F32 = jnp.float32
BF16 = jnp.bfloat16
VMEM_LIMIT = 48 * 2**20
PREPARE_VMEM_LIMIT = 54912 * 2**10


def tables():
    j = np.arange(B)
    angle = (j[:, None] * j[None, :] % B) * (2.0 * np.pi / B)
    c, s = np.cos(angle), np.sin(angle)
    right = np.zeros((2 * B, 2 * B))
    for half, start in ((0, 0), (1, H)):
        right[start : start + B, half * H : half * H + H] = c[:, :H]
        right[start : start + B, B + half * H : B + half * H + H] = s[:, :H]
    left = np.block([[c, -s], [-s, -c]])
    q = np.arange((PAIRS + 1) * B)
    sign = 1.0 - 2.0 * (q % 2)
    middle = np.zeros(((PAIRS + 1) * B, B))
    for m in range(PAIRS):
        middle[:, m] = sign * (q // B == m)
        middle[:, H + m] = sign * ((q - H) // B == m)
    back_left = np.block([[c, -s], [s, c]])
    twice = np.where(j[:H] == 0, 1.0, 2.0)[:, None] / B
    back_right = np.zeros((2 * B, 2 * B))
    imag = -twice * s[:H]
    imag[0] = (1.0 - 2.0 * (j % 2)) / B
    for half in range(2):
        lanes = slice(half * B, half * B + B)
        back_right[half * H : half * H + H, lanes] = twice * c[:H]
        back_right[B + half * H : B + half * H + H, lanes] = imag
    return tuple(np.asarray(t, np.float32).astype(BF16) for t in (right, left, middle, back_left, back_right))


def dot(a, b):
    return jnp.dot(a, b, preferred_element_type=F32)


def shifted(x, off):
    rows = x.shape[0]
    if off == 0:
        return x
    gap = jnp.zeros((rows, abs(off)), x.dtype)
    if off > 0:
        return jnp.concatenate([x[:, off:], gap], 1)
    return jnp.concatenate([gap, x[:, :off]], 1)


def banded(taps_ref, which, valid):
    high, low = [], []
    for b in range(5):
        band = jnp.zeros(which.shape, F32)
        for a in range(5):
            band = jnp.where(which == a, taps_ref[0, 0, 5 * a + b], band)
        if valid is not None:
            band = jnp.where(valid, band, 0.0)
        top = band.astype(BF16)
        high.append(top)
        low.append((band - top.astype(F32)).astype(BF16))
    return jnp.concatenate([jnp.concatenate(high, 1), jnp.concatenate(low, 1)], 0)


def prepare_kernel(image, inner, outer, sems):
    last = image.shape[1] - EDGE
    odd = lax.rem(lax.axis_index("tile"), 2)
    to_inner = pltpu.make_async_copy(image.at[0, pl.ds(pl.multiple_of((1 - odd) * last, EDGE), EDGE)], inner, sems.at[0])
    to_outer = pltpu.make_async_copy(image.at[0, pl.ds(pl.multiple_of(odd * last, EDGE), EDGE)], outer, sems.at[1])
    to_inner.start()
    to_outer.start()
    to_inner.wait()
    to_outer.wait()


def lens_kernel(taps_ref, image_ref, weight_ref, blocks_ref, edge_ref):
    x = image_ref[0]
    rows, cols = x.shape
    across = cols // B
    i = lax.broadcasted_iota(jnp.int32, (rows, rows), 0)
    j = lax.broadcasted_iota(jnp.int32, (rows, rows), 1)
    bands = banded(taps_ref, j - i + 2, None)
    stack = jnp.concatenate([shifted(x, b - 2) for b in range(5)], 0)
    both = dot(bands, stack)
    corrected = both[:rows] + both[rows:]
    edge_ref[:EDGE] = corrected[:EDGE]
    edge_ref[EDGE:] = corrected[rows - EDGE :]
    weighted = (corrected * weight_ref[0].astype(F32)).astype(BF16)
    for k in range(rows // B * across):
        r, c = k // across * B, k % across * B
        blocks_ref[k] = weighted[r : r + B, c : c + B]


def pick_kernel(
    taps_ref, src_ref, count_ref, inner_ref, outer_ref, edge_ref, weight_ref, blocks_ref, anchor_ref, out, first_ref, zero_ref, fixed_ref, sems
):
    rows, cols = weight_ref.shape[1:]
    across = cols // B
    count = rows // B * across
    zero_ref[...] = jnp.zeros((B, B), BF16)
    fixed_ref[count] = jnp.zeros((EDGE, B), BF16)
    first_ref[0] = anchor_ref[0]
    inside = B - EDGE
    sends, edges = [], []
    for d in range(out.shape[0]):
        for q in range(out.shape[1]):
            live = q < count_ref[0, 0, d]
            block = src_ref[0, 0, d, q]
            upper = block < across
            at = pl.multiple_of(jnp.where(upper, EDGE, 0), EDGE)
            edges.append((d, q, jnp.where(live, block, count), pl.multiple_of(jnp.where(upper, 0, inside), EDGE)))
            here = out.at[d, q, pl.ds(at, inside), :]
            sends.append(pltpu.make_async_copy(blocks_ref.at[block, pl.ds(at, inside), :], here, sems.at[0, d, q]))

            @pl.when(live)
            def _(send=sends[-1]):
                send.start()

            @pl.when(jnp.logical_not(live))
            def _(here=here, d=d, q=q):
                pltpu.make_async_copy(zero_ref.at[pl.ds(0, inside), :], here, sems.at[0, d, q]).start()

    e = lax.broadcasted_iota(jnp.int32, (2 * EDGE, 2 * EDGE), 0)
    k = lax.broadcasted_iota(jnp.int32, (2 * EDGE, 2 * EDGE), 1)
    upper = (e < EDGE) & (k < EDGE)
    lower = (e >= EDGE) & (k >= EDGE)
    which = jnp.where(upper, k - (EDGE - 2) - e, k + (EDGE + 2) - e)
    odd = lax.rem(lax.axis_index("tile"), 2) == 1
    inner, outer = inner_ref[...], outer_ref[...]
    rim = jnp.concatenate([jnp.where(odd, inner, outer), jnp.where(odd, outer, inner)], 0)
    rims = jnp.concatenate([shifted(rim, b - 2) for b in range(5)], 0)
    both = dot(banded(taps_ref, which, upper | lower), rims)
    corrected = edge_ref[...] + (both[: 2 * EDGE] + both[2 * EDGE :])
    top = (corrected[:EDGE] * weight_ref[0, :EDGE].astype(F32)).astype(BF16)
    bottom = (corrected[EDGE:] * weight_ref[0, rows - EDGE :].astype(F32)).astype(BF16)
    for c in range(across):
        fixed_ref[c] = top[:, c * B : c * B + B]
        fixed_ref[count - across + c] = bottom[:, c * B : c * B + B]
    for d, q, which, at in edges:
        sends.append(pltpu.make_async_copy(fixed_ref.at[which], out.at[d, q, pl.ds(at, EDGE), :], sems.at[1, d, q]))
        sends[-1].start()
    for send in sends:
        send.wait()


def strip_kernel(dst_ref, in_ref, a_ref, rest_ref, acc_ref):
    acc_ref[...] = jnp.zeros_like(acc_ref)
    for d in range(in_ref.shape[0]):
        for q in range(in_ref.shape[1]):
            j = dst_ref[0, d, 0, q]
            acc_ref[j] = acc_ref[j] + in_ref[d, q].astype(F32)
    a_ref[...] = acc_ref[:EARLY].astype(BF16)
    rest_ref[...] = acc_ref[EARLY:]


def rest_kernel(a_ref, rest_ref, b_ref, first_ref):
    b_ref[...] = rest_ref[...].astype(BF16)
    first_ref[0] = a_ref[0]


def forward(blocks, right, left, middle):
    pairs = len(blocks) - 1
    both = jnp.concatenate([jnp.concatenate([blocks[m], blocks[m + 1]], 1) for m in range(pairs)], 0)
    p = dot(both, right).astype(BF16)
    re = [p[m * B : m * B + B, :B] for m in range(pairs)]
    im = [p[m * B : m * B + B, B:] for m in range(pairs)]
    spectra = dot(left, jnp.concatenate([jnp.concatenate(re, 1), jnp.concatenate(im, 1)], 0))
    p = dot(jnp.concatenate(blocks, 1), middle[: (pairs + 1) * B]).astype(BF16)
    return spectra, dot(left[:, :B], p)


def spectra_out(blocks, right_ref, left_ref, middle_ref, out_ref):
    spectra, rest = forward(blocks, right_ref[...], left_ref[...], middle_ref[...])
    out_ref[:, : spectra.shape[1]] = spectra.astype(BF16)
    out_ref[:, spectra.shape[1] :] = rest.astype(BF16)


def early_kernel(a_ref, *refs):
    spectra_out([a_ref[m] for m in range(EARLY)], *refs)


def late_kernel(a_ref, b_ref, rim_ref, *refs):
    spectra_out([a_ref[EARLY - 1]] + [b_ref[m] for m in range(b_ref.shape[0])] + [rim_ref[0]], *refs)


def correlate_chunk(cur_ref, blocks, tables, out, at, cross_ref, mag_ref, result_ref, sems):
    right, left, middle, back_left, back_right = (table[...] for table in tables)
    pairs = len(blocks) - 1
    lane = lax.broadcasted_iota(jnp.int32, (1, B), 1)
    twice = jnp.where(lane % H == 0, 1.0, 2.0)
    sums = []
    spectra, rest = forward(blocks, right, left, middle)
    for m in range(pairs + 1):
        f = spectra[:, m * B : m * B + B] if m < pairs else rest
        c = cur_ref[:, m * B : m * B + B].astype(F32)
        ar, ai, br, bi = c[:B], c[B:], f[:B], f[B:]
        re = ar * br + ai * bi
        im = ai * br - ar * bi
        square = re * re + im * im
        mag = square * lax.rsqrt(jnp.maximum(square, 1e-30))
        cross_ref[m, :B] = re
        cross_ref[m, B:] = im
        mag_ref[m] = mag
        total = jnp.sum(mag, axis=0, keepdims=True)
        sums.append(total * twice if m < pairs else total)
    row = lax.broadcasted_iota(jnp.int32, (pairs, B), 0)
    lanes = lax.broadcasted_iota(jnp.int32, (pairs, B), 1)
    mine = row == lanes % H
    table = jnp.concatenate(sums[:pairs], 0) + jnp.where(mine, sums[pairs], 0.0)
    aligned = lanes < H
    first = jnp.sum(jnp.where(aligned, table, 0.0), axis=1, keepdims=True)
    second = jnp.sum(jnp.where(aligned, 0.0, table), axis=1, keepdims=True)
    floor = jnp.where(aligned, first, second) * (0.1 / (B * B)) + 1e-6
    floor_middle = jnp.sum(jnp.where(mine, floor, 0.0), axis=0, keepdims=True)
    floor_middle = jnp.where(lane % H < pairs, floor_middle, 1.0)

    def whitened(m, low):
        scale = 1.0 / (mag_ref[m] + low)
        return jnp.concatenate([cross_ref[m, :B] * scale, cross_ref[m, B:] * scale], 0).astype(BF16)

    y_middle = dot(back_left[:B], whitened(pairs, floor_middle))
    y = dot(back_left, jnp.concatenate([whitened(m, floor[m : m + 1]) for m in range(pairs)], 1))
    is_zero = lane % H == 0
    both = []
    for m in range(pairs):
        turned = y_middle if m == 0 else pltpu.roll(y_middle, B - m, 1)
        imag = jnp.where(is_zero, turned, y[B:, m * B : m * B + B])
        both.append(jnp.concatenate([y[:B, m * B : m * B + B].astype(BF16), imag.astype(BF16)], 1))
    result = dot(jnp.concatenate(both, 0), back_right)
    sends = []
    for m in range(pairs):
        result_ref[2 * m] = result[m * B : m * B + B, :B]
        result_ref[2 * m + 1] = result[m * B : m * B + B, B:]
        sends.append(
            pltpu.make_async_copy(result_ref.at[pl.ds(2 * m, 2)], out.at[0, pl.ds(2 * (at + m), 2)], sems.at[m])
        )
        sends[-1].start()
    for send in sends:
        send.wait()


def correlate_early(cur_ref, a_ref, anchor_ref, *refs):
    is_first = lax.axis_index("sec") == 0
    blocks = [jnp.where(is_first, anchor_ref[m], a_ref[m]) for m in range(EARLY)]
    correlate_chunk(cur_ref, blocks, refs[:5], refs[5], 0, *refs[6:])


def correlate_late(held, cur_ref, a_ref, b_ref, rim_ref, anchor_ref, border_ref, *refs):
    del held
    is_first = lax.axis_index("sec") == 0
    blocks = [jnp.where(is_first, anchor_ref[EARLY - 1], a_ref[EARLY - 1])]
    blocks += [jnp.where(is_first, anchor_ref[EARLY + m], b_ref[m]) for m in range(b_ref.shape[0])]
    blocks += [jnp.where(is_first, border_ref[0], rim_ref[0])]
    correlate_chunk(cur_ref, blocks, refs[:5], refs[5], EARLY - 1, *refs[6:])


SMEM = pl.BlockSpec(memory_space=pltpu.SMEM)
VMEM = pl.BlockSpec(memory_space=pltpu.VMEM)
ANY = pl.BlockSpec(memory_space=pl.ANY)
HBM = pl.BlockSpec(memory_space=pltpu.HBM)


def call(kernel, out_shape, in_specs, out_specs, scratch, flops, moved, args, aliases=None, grid=None, limit=VMEM_LIMIT):
    extra = {} if grid is None else {"grid": grid}
    return pl.pallas_call(
        kernel,
        out_shape=out_shape,
        in_specs=in_specs,
        out_specs=out_specs,
        scratch_shapes=scratch,
        input_output_aliases=aliases or {},
        compiler_params=pltpu.CompilerParams(vmem_limit_bytes=limit),
        cost_estimate=pl.CostEstimate(flops=flops, bytes_accessed=moved, transcendentals=0),
        **extra,
    )(*args)


def body(image, weight, lens_filter_taps, block_src, block_dst, valid_count, anchor):
    rows, cols = image.shape[1:]
    strips = lax.axis_size("tile")
    sections = lax.axis_size("sec")
    slots = block_src.shape[-1]
    count = anchor.shape[0]
    shape = jax.ShapeDtypeStruct
    whole = lambda *dims: pl.BlockSpec(dims, lambda i: (0,) * len(dims))
    back = [(i + 1, i) for i in range(strips - 1)]
    inner, outer = call(
        prepare_kernel,
        (shape((EDGE, cols), BF16), shape((EDGE, cols), BF16)),
        [HBM],
        (VMEM,) * 2,
        [pltpu.SemaphoreType.DMA((2,))],
        2**33,
        2**17,
        (image,),
        limit=PREPARE_VMEM_LIMIT,
    )
    inner = lax.ppermute(inner, "tile", [(t, t ^ 1) for t in range(strips)])
    outer = lax.ppermute(outer, "tile", [(t, t + 2 * (t % 2) - 1) for t in range(1, strips - 1)])
    tile_blocks = rows // B * (cols // B)
    blocks, edge = call(
        lens_kernel,
        (shape((tile_blocks, B, B), BF16), shape((2 * EDGE, cols), F32)),
        [SMEM, VMEM, VMEM],
        (VMEM, VMEM),
        [],
        2 * 10 * rows * rows * cols,
        3 * 2 * rows * cols,
        (lens_filter_taps, image, weight),
    )
    outgoing, anchor_first = call(
        pick_kernel,
        (shape((strips, slots, B, B), BF16), shape((1, B, B), BF16)),
        [SMEM] * 3 + [VMEM] * 6,
        (HBM, VMEM),
        [
            pltpu.VMEM((B, B), BF16),
            pltpu.VMEM((tile_blocks + 1, EDGE, B), BF16),
            pltpu.SemaphoreType.DMA((2, strips, slots)),
        ],
        2**20,
        4 * 2 * rows * cols,
        (lens_filter_taps, block_src, valid_count, inner, outer, edge, weight, blocks, anchor),
    )
    incoming = lax.all_to_all(outgoing, "tile", split_axis=0, concat_axis=0, tiled=True)
    border = lax.ppermute(anchor_first, "tile", back)
    incoming, border = lax.optimization_barrier((incoming, border))
    part_a, rest = call(
        strip_kernel,
        (shape((EARLY, B, B), BF16), shape((count - EARLY, B, B), F32)),
        [SMEM, VMEM],
        (VMEM, VMEM),
        [pltpu.VMEM((count, B, B), F32)],
        2**20,
        4 * 2 * rows * cols,
        (block_dst, incoming),
    )
    part_b, first = call(
        rest_kernel,
        (shape((count - EARLY, B, B), BF16), shape((1, B, B), BF16)),
        [VMEM] * 2,
        (VMEM, VMEM),
        [],
        2**18,
        6 * EARLY * B * B,
        (part_a, rest),
    )
    on = [(i, i + 1) for i in range(sections - 1)]
    prior_a = lax.ppermute(part_a, "sec", on)
    prior_b = lax.ppermute(part_b, "sec", on)
    own_rim = lax.ppermute(first, "tile", back)
    across = [(s * strips + d + 1, (s + 1) * strips + d) for s in range(sections - 1) for d in range(strips - 1)]
    prior_rim = lax.ppermute(first, ("sec", "tile"), across)
    right, left, middle, back_left, back_right = (jnp.asarray(t) for t in tables())
    early, late = EARLY - 1, count - EARLY + 1
    current = lambda kernel, pairs, *parts: call(
        kernel,
        shape((2 * B, (pairs + 1) * B), BF16),
        [VMEM] * (len(parts) + 3),
        VMEM,
        [],
        2**10,
        2**10,
        (*parts, right, left, middle),
    )
    spectra_a = current(early_kernel, early, part_a)
    spectra_b = current(late_kernel, late, part_a, part_b, own_rim)
    result = shape((1, 2 * count, B, B), F32)
    scratch = lambda pairs: [
        pltpu.VMEM((pairs + 1, 2 * B, B), F32),
        pltpu.VMEM((pairs + 1, B, B), F32),
        pltpu.VMEM((2 * pairs, B, B), F32),
        pltpu.SemaphoreType.DMA((pairs,)),
    ]
    held = call(
        correlate_early,
        result,
        [VMEM] * 8,
        HBM,
        scratch(early),
        2**10,
        2**10,
        (spectra_a, prior_a, anchor, right, left, middle, back_left, back_right),
    )
    return call(
        correlate_late,
        result,
        [HBM] + [VMEM] * 11,
        HBM,
        scratch(late),
        2**30,
        2**22,
        (held, spectra_b, prior_a, prior_b, prior_rim, anchor, border, right, left, middle, back_left, back_right),
        aliases={0: 0},
    )


def solution(mesh):
    in_specs = (
        P("sec", "tile", None),
        P("sec", "tile", None),
        P("sec", "tile", None),
        P("sec", "tile", None, None),
        P("sec", None, "tile", None),
        P("sec", "tile", None),
        P("tile", None, None),
    )
    out_specs = P("sec", "tile", None, None)
    return jax.shard_map(body, mesh=mesh, in_specs=in_specs, out_specs=out_specs, check_vma=False)
```

```python
import jax
import jax.numpy as jnp
import numpy as np
from jax import lax
from jax.experimental import pallas as pl
from jax.experimental.pallas import tpu as pltpu
from jax.sharding import PartitionSpec as P

B = 128
H = B // 2
EDGE = 16
EARLY = 11
PAIRS = 10
F32 = jnp.float32
BF16 = jnp.bfloat16
VMEM_LIMIT = 48 * 2**20
PREPARE_VMEM_LIMIT = 54912 * 2**10


def tables():
    j = np.arange(B)
    angle = (j[:, None] * j[None, :] % B) * (2.0 * np.pi / B)
    c, s = np.cos(angle), np.sin(angle)
    right = np.zeros((2 * B, 2 * B))
    for half, start in ((0, 0), (1, H)):
        right[start : start + B, half * H : half * H + H] = c[:, :H]
        right[start : start + B, B + half * H : B + half * H + H] = s[:, :H]
    left = np.block([[c, -s], [-s, -c]])
    q = np.arange((PAIRS + 1) * B)
    sign = 1.0 - 2.0 * (q % 2)
    middle = np.zeros(((PAIRS + 1) * B, B))
    for m in range(PAIRS):
        middle[:, m] = sign * (q // B == m)
        middle[:, H + m] = sign * ((q - H) // B == m)
    back_left = np.block([[c, -s], [s, c]])
    twice = np.where(j[:H] == 0, 1.0, 2.0)[:, None] / B
    back_right = np.zeros((2 * B, 2 * B))
    imag = -twice * s[:H]
    imag[0] = (1.0 - 2.0 * (j % 2)) / B
    for half in range(2):
        lanes = slice(half * B, half * B + B)
        back_right[half * H : half * H + H, lanes] = twice * c[:H]
        back_right[B + half * H : B + half * H + H, lanes] = imag
    return tuple(np.asarray(t, np.float32).astype(BF16) for t in (right, left, middle, back_left, back_right))


def dot(a, b):
    return jnp.dot(a, b, preferred_element_type=F32)


def shifted(x, off):
    rows = x.shape[0]
    if off == 0:
        return x
    gap = jnp.zeros((rows, abs(off)), x.dtype)
    if off > 0:
        return jnp.concatenate([x[:, off:], gap], 1)
    return jnp.concatenate([gap, x[:, :off]], 1)


def banded(taps_ref, which, valid):
    high, low = [], []
    for b in range(5):
        band = jnp.zeros(which.shape, F32)
        for a in range(5):
            band = jnp.where(which == a, taps_ref[0, 0, 5 * a + b], band)
        if valid is not None:
            band = jnp.where(valid, band, 0.0)
        top = band.astype(BF16)
        high.append(top)
        low.append((band - top.astype(F32)).astype(BF16))
    return jnp.concatenate([jnp.concatenate(high, 1), jnp.concatenate(low, 1)], 0)


def prepare_kernel(image, inner, outer, sems):
    last = image.shape[1] - EDGE
    odd = lax.rem(lax.axis_index("tile"), 2)
    to_inner = pltpu.make_async_copy(image.at[0, pl.ds(pl.multiple_of((1 - odd) * last, EDGE), EDGE)], inner, sems.at[0])
    wide = outer.shape[0]
    last = image.shape[1] - wide
    to_outer = pltpu.make_async_copy(image.at[0, pl.ds(pl.multiple_of(odd * last, EDGE), wide)], outer, sems.at[1])
    to_inner.start()
    to_outer.start()
    to_inner.wait()
    to_outer.wait()


def edge_bands(taps_ref):
    e = lax.broadcasted_iota(jnp.int32, (2 * EDGE, 2 * EDGE), 0)
    k = lax.broadcasted_iota(jnp.int32, (2 * EDGE, 2 * EDGE), 1)
    upper = (e < EDGE) & (k < EDGE)
    lower = (e >= EDGE) & (k >= EDGE)
    return banded(taps_ref, jnp.where(upper, k - (EDGE - 2) - e, k + (EDGE + 2) - e), upper | lower)


def lens_kernel(taps_ref, image_ref, weight_ref, blocks_ref, edge_ref, bands_ref):
    x = image_ref[0]
    rows, cols = x.shape
    across = cols // B
    i = lax.broadcasted_iota(jnp.int32, (B, B), 0)
    j = lax.broadcasted_iota(jnp.int32, (B, B), 1)
    bands = banded(taps_ref, j - i + 2, None)
    columns = [shifted(x, b - 2) for b in range(5)]
    stack = jnp.concatenate([jnp.concatenate([c[:B] for c in columns], 0), jnp.concatenate([c[B:] for c in columns], 0)], 1)
    both = dot(bands, stack)
    main = both[:B] + both[B:]
    edges = edge_bands(taps_ref)
    bands_ref[...] = edges
    both = dot(edges, jnp.concatenate([c[B - EDGE : B + EDGE] for c in columns], 0))
    middle = both[: 2 * EDGE] + both[2 * EDGE :]
    corrected = jnp.concatenate(
        [
            main[: B - EDGE, :cols],
            main[B - EDGE :, :cols] + middle[EDGE:],
            main[:EDGE, cols:] + middle[:EDGE],
            main[EDGE:, cols:],
        ],
        0,
    )
    edge_ref[:EDGE] = corrected[:EDGE]
    edge_ref[EDGE:] = corrected[rows - EDGE :]
    weighted = (corrected * weight_ref[0].astype(F32)).astype(BF16)
    for k in range(rows // B * across):
        r, c = k // across * B, k % across * B
        blocks_ref[k] = weighted[r : r + B, c : c + B]


def pick_kernel(
    bands_ref, src_ref, count_ref, inner_ref, outer_ref, edge_ref, weight_ref, blocks_ref, dst_ref, out, dst_out, fixed_ref
):
    dst_out[...] = dst_ref[...]
    rows, cols = weight_ref.shape[1:]
    across = cols // B
    count = rows // B * across
    places = []
    for d in range(out.shape[0]):
        for q in range(out.shape[1]):
            live = q < count_ref[0, 0, d]
            block = src_ref[0, 0, d, q]
            out[d, q] = jnp.where(live, blocks_ref[block], jnp.zeros((), BF16))
            places.append((d, q, live, block))
    odd = lax.rem(lax.axis_index("tile"), 2) == 1
    inner, outer = inner_ref[...], outer_ref[...]
    rim = jnp.concatenate([jnp.where(odd, inner, outer[EDGE:]), jnp.where(odd, outer[:EDGE], inner)], 0)
    rims = jnp.concatenate([shifted(rim, b - 2) for b in range(5)], 0)
    both = dot(bands_ref[...], rims)
    corrected = edge_ref[...] + (both[: 2 * EDGE] + both[2 * EDGE :])
    top = (corrected[:EDGE] * weight_ref[0, :EDGE].astype(F32)).astype(BF16)
    bottom = (corrected[EDGE:] * weight_ref[0, rows - EDGE :].astype(F32)).astype(BF16)
    for c in range(across):
        fixed_ref[c] = top[:, c * B : c * B + B]
        fixed_ref[count - across + c] = bottom[:, c * B : c * B + B]
    for d, q, live, block in places:
        at = pl.multiple_of(jnp.where(block < across, 0, B - EDGE), EDGE)
        out[d, q, pl.ds(at, EDGE), :] = jnp.where(live, fixed_ref[block], jnp.zeros((), BF16))


def strip_kernel(dst_ref, in_ref, a_ref, rest_ref, acc_ref):
    acc_ref[...] = jnp.zeros_like(acc_ref)
    for d in range(in_ref.shape[0]):
        for q in range(in_ref.shape[1]):
            j = dst_ref[0, d, 0, q]
            acc_ref[j] = acc_ref[j] + in_ref[d, q].astype(F32)
    a_ref[...] = acc_ref[:EARLY].astype(BF16)
    rest_ref[...] = acc_ref[EARLY:]


def rest_kernel(a_ref, rest_ref, anchor_ref, b_ref, first_ref, anchor_first_ref):
    b_ref[...] = rest_ref[...].astype(BF16)
    first_ref[0] = a_ref[0]
    anchor_first_ref[0] = anchor_ref[0]


def forward(blocks, right, left, middle):
    pairs = len(blocks) - 1
    both = jnp.concatenate([jnp.concatenate([blocks[m], blocks[m + 1]], 1) for m in range(pairs)], 0)
    p = dot(both, right).astype(BF16)
    re = [p[m * B : m * B + B, :B] for m in range(pairs)]
    im = [p[m * B : m * B + B, B:] for m in range(pairs)]
    spectra = dot(left, jnp.concatenate([jnp.concatenate(re, 1), jnp.concatenate(im, 1)], 0))
    p = dot(jnp.concatenate(blocks, 1), middle[: (pairs + 1) * B]).astype(BF16)
    return spectra, dot(left[:, :B], p)


def spectra_out(blocks, right_ref, left_ref, middle_ref, out_ref):
    spectra, rest = forward(blocks, right_ref[...], left_ref[...], middle_ref[...])
    out_ref[:, : spectra.shape[1]] = spectra.astype(BF16)
    out_ref[:, spectra.shape[1] :] = rest.astype(BF16)


def early_kernel(a_ref, *refs):
    spectra_out([a_ref[m] for m in range(EARLY)], *refs)


def late_kernel(a_ref, b_ref, rim_ref, *refs):
    spectra_out([a_ref[EARLY - 1]] + [b_ref[m] for m in range(b_ref.shape[0])] + [rim_ref[0]], *refs)


def correlate_chunk(cur_ref, blocks, tables, out, at, cross_ref, mag_ref, result_ref, sems):
    right, left, middle, back_left, back_right = (table[...] for table in tables)
    pairs = len(blocks) - 1
    lane = lax.broadcasted_iota(jnp.int32, (1, B), 1)
    twice = jnp.where(lane % H == 0, 1.0, 2.0)
    sums = []
    spectra, rest = forward(blocks, right, left, middle)
    for m in range(pairs + 1):
        f = spectra[:, m * B : m * B + B] if m < pairs else rest
        c = cur_ref[:, m * B : m * B + B].astype(F32)
        ar, ai, br, bi = c[:B], c[B:], f[:B], f[B:]
        re = ar * br + ai * bi
        im = ai * br - ar * bi
        square = re * re + im * im
        mag = square * lax.rsqrt(jnp.maximum(square, 1e-30))
        cross_ref[m, :B] = re
        cross_ref[m, B:] = im
        mag_ref[m] = mag
        total = jnp.sum(mag, axis=0, keepdims=True)
        sums.append(total * twice if m < pairs else total)
    row = lax.broadcasted_iota(jnp.int32, (pairs, B), 0)
    lanes = lax.broadcasted_iota(jnp.int32, (pairs, B), 1)
    mine = row == lanes % H
    table = jnp.concatenate(sums[:pairs], 0) + jnp.where(mine, sums[pairs], 0.0)
    aligned = lanes < H
    first = jnp.sum(jnp.where(aligned, table, 0.0), axis=1, keepdims=True)
    second = jnp.sum(jnp.where(aligned, 0.0, table), axis=1, keepdims=True)
    floor = jnp.where(aligned, first, second) * (0.1 / (B * B)) + 1e-6
    floor_middle = jnp.sum(jnp.where(mine, floor, 0.0), axis=0, keepdims=True)
    floor_middle = jnp.where(lane % H < pairs, floor_middle, 1.0)

    def whitened(m, low):
        scale = 1.0 / (mag_ref[m] + low)
        return jnp.concatenate([cross_ref[m, :B] * scale, cross_ref[m, B:] * scale], 0).astype(BF16)

    y_middle = dot(back_left[:B], whitened(pairs, floor_middle))
    y = dot(back_left, jnp.concatenate([whitened(m, floor[m : m + 1]) for m in range(pairs)], 1))
    is_zero = lane % H == 0
    both = []
    for m in range(pairs):
        turned = y_middle if m == 0 else pltpu.roll(y_middle, B - m, 1)
        imag = jnp.where(is_zero, turned, y[B:, m * B : m * B + B])
        both.append(jnp.concatenate([y[:B, m * B : m * B + B].astype(BF16), imag.astype(BF16)], 1))
    result = dot(jnp.concatenate(both, 0), back_right)
    sends = []
    for m in range(pairs):
        result_ref[2 * m] = result[m * B : m * B + B, :B]
        result_ref[2 * m + 1] = result[m * B : m * B + B, B:]
        sends.append(
            pltpu.make_async_copy(result_ref.at[pl.ds(2 * m, 2)], out.at[0, pl.ds(2 * (at + m), 2)], sems.at[m])
        )
        sends[-1].start()
    for send in sends:
        send.wait()


def correlate_early(cur_ref, a_ref, anchor_ref, *refs):
    is_first = lax.axis_index("sec") == 0
    blocks = [jnp.where(is_first, anchor_ref[m], a_ref[m]) for m in range(EARLY)]
    correlate_chunk(cur_ref, blocks, refs[:5], refs[5], 0, *refs[6:])


def correlate_late(held, cur_ref, a_ref, b_ref, rim_ref, anchor_ref, border_ref, *refs):
    del held
    is_first = lax.axis_index("sec") == 0
    blocks = [jnp.where(is_first, anchor_ref[EARLY - 1], a_ref[EARLY - 1])]
    blocks += [jnp.where(is_first, anchor_ref[EARLY + m], b_ref[m]) for m in range(b_ref.shape[0])]
    blocks += [jnp.where(is_first, border_ref[0], rim_ref[0])]
    correlate_chunk(cur_ref, blocks, refs[:5], refs[5], EARLY - 1, *refs[6:])


SMEM = pl.BlockSpec(memory_space=pltpu.SMEM)
VMEM = pl.BlockSpec(memory_space=pltpu.VMEM)
ANY = pl.BlockSpec(memory_space=pl.ANY)
HBM = pl.BlockSpec(memory_space=pltpu.HBM)


def call(kernel, out_shape, in_specs, out_specs, scratch, flops, moved, args, aliases=None, grid=None, limit=VMEM_LIMIT):
    extra = {} if grid is None else {"grid": grid}
    return pl.pallas_call(
        kernel,
        out_shape=out_shape,
        in_specs=in_specs,
        out_specs=out_specs,
        scratch_shapes=scratch,
        input_output_aliases=aliases or {},
        compiler_params=pltpu.CompilerParams(vmem_limit_bytes=limit),
        cost_estimate=pl.CostEstimate(flops=flops, bytes_accessed=moved, transcendentals=0),
        **extra,
    )(*args)


def body(image, weight, lens_filter_taps, block_src, block_dst, valid_count, anchor):
    rows, cols = image.shape[1:]
    strips = lax.axis_size("tile")
    sections = lax.axis_size("sec")
    slots = block_src.shape[-1]
    count = anchor.shape[0]
    shape = jax.ShapeDtypeStruct
    whole = lambda *dims: pl.BlockSpec(dims, lambda i: (0,) * len(dims))
    back = [(i + 1, i) for i in range(strips - 1)]
    inner, outer = call(
        prepare_kernel,
        (shape((EDGE, cols), BF16), shape((2 * EDGE, cols), BF16)),
        [HBM],
        (VMEM,) * 2,
        [pltpu.SemaphoreType.DMA((2,))],
        2**33,
        2**17,
        (image,),
        limit=PREPARE_VMEM_LIMIT,
    )
    outer = lax.ppermute(outer, "tile", [(t, t + 2 * (t % 2) - 1) for t in range(1, strips - 1)])
    inner = lax.ppermute(inner, "tile", [(t, t ^ 1) for t in range(strips)])
    tile_blocks = rows // B * (cols // B)
    blocks, edge, bands = call(
        lens_kernel,
        (shape((tile_blocks, B, B), BF16), shape((2 * EDGE, cols), F32), shape((4 * EDGE, 10 * EDGE), BF16)),
        [SMEM, VMEM, VMEM],
        (VMEM, VMEM, VMEM),
        [],
        2**10,
        2**10,
        (lens_filter_taps, image, weight),
    )
    outgoing, places = call(
        pick_kernel,
        (shape((strips, slots, B, B), BF16), shape((1, strips, 1, slots), jnp.int32)),
        [VMEM, SMEM, SMEM] + [VMEM] * 6,
        (VMEM, VMEM),
        [pltpu.VMEM((tile_blocks, EDGE, B), BF16)],
        2**20,
        4 * 2 * rows * cols,
        (bands, block_src, valid_count, inner, outer, edge, weight, blocks, block_dst),
    )
    incoming = lax.all_to_all(outgoing, "tile", split_axis=0, concat_axis=0, tiled=True)
    part_a, rest = call(
        strip_kernel,
        (shape((EARLY, B, B), BF16), shape((count - EARLY, B, B), F32)),
        [SMEM, VMEM],
        (VMEM, VMEM),
        [pltpu.VMEM((count, B, B), F32)],
        2**20,
        4 * 2 * rows * cols,
        (places, incoming),
    )
    part_b, first, anchor_first = call(
        rest_kernel,
        (shape((count - EARLY, B, B), BF16), shape((1, B, B), BF16), shape((1, B, B), BF16)),
        [VMEM] * 3,
        (VMEM, VMEM, VMEM),
        [],
        2**18,
        6 * EARLY * B * B,
        (part_a, rest, anchor),
    )
    on = [(i, i + 1) for i in range(sections - 1)]
    prior_a = lax.ppermute(part_a, "sec", on)
    prior_b = lax.ppermute(part_b, "sec", on)
    own_rim = lax.ppermute(first, "tile", back)
    across = [(s * strips + d + 1, (s + 1) * strips + d) for s in range(sections - 1) for d in range(strips - 1)]
    prior_rim = lax.ppermute(first, ("sec", "tile"), across)
    border = lax.ppermute(anchor_first, "tile", back)
    right, left, middle, back_left, back_right = (jnp.asarray(t) for t in tables())
    early, late = EARLY - 1, count - EARLY + 1
    current = lambda kernel, pairs, *parts: call(
        kernel,
        shape((2 * B, (pairs + 1) * B), BF16),
        [VMEM] * (len(parts) + 3),
        VMEM,
        [],
        2**10,
        2**10,
        (*parts, right, left, middle),
    )
    spectra_a = current(early_kernel, early, part_a)
    spectra_b = current(late_kernel, late, part_a, part_b, own_rim)
    result = shape((1, 2 * count, B, B), F32)
    scratch = lambda pairs: [
        pltpu.VMEM((pairs + 1, 2 * B, B), F32),
        pltpu.VMEM((pairs + 1, B, B), F32),
        pltpu.VMEM((2 * pairs, B, B), F32),
        pltpu.SemaphoreType.DMA((pairs,)),
    ]
    held = call(
        correlate_early,
        result,
        [VMEM] * 8,
        HBM,
        scratch(early),
        2**10,
        2**10,
        (spectra_a, prior_a, anchor, right, left, middle, back_left, back_right),
    )
    return call(
        correlate_late,
        result,
        [HBM] + [VMEM] * 11,
        HBM,
        scratch(late),
        2**30,
        2**22,
        (held, spectra_b, prior_a, prior_b, prior_rim, anchor, border, right, left, middle, back_left, back_right),
        aliases={0: 0},
    )


def solution(mesh):
    in_specs = (
        P("sec", "tile", None),
        P("sec", "tile", None),
        P("sec", "tile", None),
        P("sec", "tile", None, None),
        P("sec", None, "tile", None),
        P("sec", "tile", None),
        P("tile", None, None),
    )
    out_specs = P("sec", "tile", None, None)
    return jax.shard_map(body, mesh=mesh, in_specs=in_specs, out_specs=out_specs, check_vma=False)
```

```python
import jax
import jax.numpy as jnp
import numpy as np
from jax import lax
from jax.experimental import pallas as pl
from jax.experimental.pallas import tpu as pltpu
from jax.sharding import PartitionSpec as P

B = 128
H = B // 2
EDGE = 16
EARLY = 11
PAIRS = 10
F32 = jnp.float32
BF16 = jnp.bfloat16
VMEM_LIMIT = 48 * 2**20
PREPARE_VMEM_LIMIT = 54912 * 2**10


def tables():
    j = np.arange(B)
    angle = (j[:, None] * j[None, :] % B) * (2.0 * np.pi / B)
    c, s = np.cos(angle), np.sin(angle)
    right = np.zeros((2 * B, 2 * B))
    for half, start in ((0, 0), (1, H)):
        right[start : start + B, half * H : half * H + H] = c[:, :H]
        right[start : start + B, B + half * H : B + half * H + H] = s[:, :H]
    left = np.block([[c, -s], [-s, -c]])
    q = np.arange((PAIRS + 1) * B)
    sign = 1.0 - 2.0 * (q % 2)
    middle = np.zeros(((PAIRS + 1) * B, B))
    for m in range(PAIRS):
        middle[:, m] = sign * (q // B == m)
        middle[:, H + m] = sign * ((q - H) // B == m)
    back_left = np.block([[c, -s], [s, c]])
    twice = np.where(j[:H] == 0, 1.0, 2.0)[:, None] / B
    back_right = np.zeros((2 * B, 2 * B))
    imag = -twice * s[:H]
    imag[0] = (1.0 - 2.0 * (j % 2)) / B
    for half in range(2):
        lanes = slice(half * B, half * B + B)
        back_right[half * H : half * H + H, lanes] = twice * c[:H]
        back_right[B + half * H : B + half * H + H, lanes] = imag
    return tuple(np.asarray(t, np.float32).astype(BF16) for t in (right, left, middle, back_left, back_right))


def dot(a, b):
    return jnp.dot(a, b, preferred_element_type=F32)


def shifted(x, off):
    rows = x.shape[0]
    if off == 0:
        return x
    gap = jnp.zeros((rows, abs(off)), x.dtype)
    if off > 0:
        return jnp.concatenate([x[:, off:], gap], 1)
    return jnp.concatenate([gap, x[:, :off]], 1)


def banded(taps_ref, which, valid):
    high, low = [], []
    for b in range(5):
        band = jnp.zeros(which.shape, F32)
        for a in range(5):
            band = jnp.where(which == a, taps_ref[0, 0, 5 * a + b], band)
        if valid is not None:
            band = jnp.where(valid, band, 0.0)
        top = band.astype(BF16)
        high.append(top)
        low.append((band - top.astype(F32)).astype(BF16))
    return jnp.concatenate([jnp.concatenate(high, 1), jnp.concatenate(low, 1)], 0)


def prepare_kernel(image, inner, outer, sems):
    last = image.shape[1] - EDGE
    odd = lax.rem(lax.axis_index("tile"), 2)
    to_inner = pltpu.make_async_copy(image.at[0, pl.ds(pl.multiple_of((1 - odd) * last, EDGE), EDGE)], inner, sems.at[0])
    wide = outer.shape[0]
    last = image.shape[1] - wide
    to_outer = pltpu.make_async_copy(image.at[0, pl.ds(pl.multiple_of(odd * last, EDGE), wide)], outer, sems.at[1])
    to_inner.start()
    to_outer.start()
    to_inner.wait()
    to_outer.wait()


def edge_bands(taps_ref):
    e = lax.broadcasted_iota(jnp.int32, (2 * EDGE, 2 * EDGE), 0)
    k = lax.broadcasted_iota(jnp.int32, (2 * EDGE, 2 * EDGE), 1)
    upper = (e < EDGE) & (k < EDGE)
    lower = (e >= EDGE) & (k >= EDGE)
    return banded(taps_ref, jnp.where(upper, k - (EDGE - 2) - e, k + (EDGE + 2) - e), upper | lower)


def lens_kernel(taps_ref, image_ref, weight_ref, blocks_ref, edge_ref, bands_ref):
    x = image_ref[0]
    rows, cols = x.shape
    across = cols // B
    i = lax.broadcasted_iota(jnp.int32, (B, B), 0)
    j = lax.broadcasted_iota(jnp.int32, (B, B), 1)
    bands = banded(taps_ref, j - i + 2, None)
    columns = [shifted(x, b - 2) for b in range(5)]
    stack = jnp.concatenate([jnp.concatenate([c[:B] for c in columns], 0), jnp.concatenate([c[B:] for c in columns], 0)], 1)
    both = dot(bands, stack)
    main = both[:B] + both[B:]
    edges = edge_bands(taps_ref)
    bands_ref[...] = edges
    both = dot(edges, jnp.concatenate([c[B - EDGE : B + EDGE] for c in columns], 0))
    middle = both[: 2 * EDGE] + both[2 * EDGE :]
    corrected = jnp.concatenate(
        [
            main[: B - EDGE, :cols],
            main[B - EDGE :, :cols] + middle[EDGE:],
            main[:EDGE, cols:] + middle[:EDGE],
            main[EDGE:, cols:],
        ],
        0,
    )
    edge_ref[:EDGE] = corrected[:EDGE]
    edge_ref[EDGE:] = corrected[rows - EDGE :]
    weighted = (corrected * weight_ref[0].astype(F32)).astype(BF16)
    for k in range(rows // B * across):
        r, c = k // across * B, k % across * B
        blocks_ref[k] = weighted[r : r + B, c : c + B]


def pick_kernel(
    bands_ref, src_ref, count_ref, inner_ref, outer_ref, edge_ref, weight_ref, blocks_ref, dst_ref, out, dst_out, fixed_ref
):
    dst_out[...] = dst_ref[...]
    rows, cols = weight_ref.shape[1:]
    across = cols // B
    count = rows // B * across
    places = []
    for d in range(out.shape[0]):
        for q in range(out.shape[1]):
            live = q < count_ref[0, 0, d]
            block = src_ref[0, 0, d, q]
            out[d, q] = jnp.where(live, blocks_ref[block], jnp.zeros((), BF16))
            places.append((d, q, live, block))
    odd = lax.rem(lax.axis_index("tile"), 2) == 1
    inner, outer = inner_ref[...], outer_ref[...]
    rim = jnp.concatenate([jnp.where(odd, inner, outer[EDGE:]), jnp.where(odd, outer[:EDGE], inner)], 0)
    rims = jnp.concatenate([shifted(rim, b - 2) for b in range(5)], 0)
    both = dot(bands_ref[...], rims)
    corrected = edge_ref[...] + (both[: 2 * EDGE] + both[2 * EDGE :])
    top = (corrected[:EDGE] * weight_ref[0, :EDGE].astype(F32)).astype(BF16)
    bottom = (corrected[EDGE:] * weight_ref[0, rows - EDGE :].astype(F32)).astype(BF16)
    for c in range(across):
        fixed_ref[c] = top[:, c * B : c * B + B]
        fixed_ref[count - across + c] = bottom[:, c * B : c * B + B]
    for d, q, live, block in places:
        at = pl.multiple_of(jnp.where(block < across, 0, B - EDGE), EDGE)
        out[d, q, pl.ds(at, EDGE), :] = jnp.where(live, fixed_ref[block], jnp.zeros((), BF16))


def strip_kernel(dst_ref, in_ref, a_ref, rest_ref, acc_ref):
    acc_ref[...] = jnp.zeros_like(acc_ref)
    for d in range(in_ref.shape[0]):
        for q in range(in_ref.shape[1]):
            j = dst_ref[0, d, 0, q]
            acc_ref[j] = acc_ref[j] + in_ref[d, q].astype(F32)
    a_ref[...] = acc_ref[:EARLY].astype(BF16)
    rest_ref[...] = acc_ref[EARLY:]


def packed_rim(block):
    return jnp.concatenate([block[:H, :H], block[H:, :H]], 1)


def unpacked_rim(rim):
    gap = jnp.zeros((H, H), rim.dtype)
    return jnp.concatenate([jnp.concatenate([rim[:, :H], gap], 1), jnp.concatenate([rim[:, H:], gap], 1)], 0)


def rest_kernel(a_ref, rest_ref, anchor_ref, b_ref, first_ref, anchor_first_ref):
    b_ref[...] = rest_ref[...].astype(BF16)
    first_ref[...] = packed_rim(a_ref[0])
    anchor_first_ref[...] = packed_rim(anchor_ref[0])


def forward(blocks, right, left, middle):
    pairs = len(blocks) - 1
    both = jnp.concatenate([jnp.concatenate([blocks[m], blocks[m + 1]], 1) for m in range(pairs)], 0)
    p = dot(both, right).astype(BF16)
    re = [p[m * B : m * B + B, :B] for m in range(pairs)]
    im = [p[m * B : m * B + B, B:] for m in range(pairs)]
    spectra = dot(left, jnp.concatenate([jnp.concatenate(re, 1), jnp.concatenate(im, 1)], 0))
    p = dot(jnp.concatenate(blocks, 1), middle[: (pairs + 1) * B]).astype(BF16)
    return spectra, dot(left[:, :B], p)


def spectra_out(blocks, right_ref, left_ref, middle_ref, out_ref):
    spectra, rest = forward(blocks, right_ref[...], left_ref[...], middle_ref[...])
    out_ref[:, : spectra.shape[1]] = spectra.astype(BF16)
    out_ref[:, spectra.shape[1] :] = rest.astype(BF16)


def early_kernel(a_ref, *refs):
    spectra_out([a_ref[m] for m in range(EARLY)], *refs)


def late_kernel(a_ref, b_ref, rim_ref, *refs):
    spectra_out([a_ref[EARLY - 1]] + [b_ref[m] for m in range(b_ref.shape[0])] + [unpacked_rim(rim_ref[...])], *refs)


def correlate_chunk(cur_ref, blocks, tables, out, at, cross_ref, mag_ref, result_ref, sems):
    right, left, middle, back_left, back_right = (table[...] for table in tables)
    pairs = len(blocks) - 1
    lane = lax.broadcasted_iota(jnp.int32, (1, B), 1)
    twice = jnp.where(lane % H == 0, 1.0, 2.0)
    sums = []
    spectra, rest = forward(blocks, right, left, middle)
    for m in range(pairs + 1):
        f = spectra[:, m * B : m * B + B] if m < pairs else rest
        c = cur_ref[:, m * B : m * B + B].astype(F32)
        ar, ai, br, bi = c[:B], c[B:], f[:B], f[B:]
        re = ar * br + ai * bi
        im = ai * br - ar * bi
        square = re * re + im * im
        mag = square * lax.rsqrt(jnp.maximum(square, 1e-30))
        cross_ref[m, :B] = re
        cross_ref[m, B:] = im
        mag_ref[m] = mag
        total = jnp.sum(mag, axis=0, keepdims=True)
        sums.append(total * twice if m < pairs else total)
    row = lax.broadcasted_iota(jnp.int32, (pairs, B), 0)
    lanes = lax.broadcasted_iota(jnp.int32, (pairs, B), 1)
    mine = row == lanes % H
    table = jnp.concatenate(sums[:pairs], 0) + jnp.where(mine, sums[pairs], 0.0)
    aligned = lanes < H
    first = jnp.sum(jnp.where(aligned, table, 0.0), axis=1, keepdims=True)
    second = jnp.sum(jnp.where(aligned, 0.0, table), axis=1, keepdims=True)
    floor = jnp.where(aligned, first, second) * (0.1 / (B * B)) + 1e-6
    floor_middle = jnp.sum(jnp.where(mine, floor, 0.0), axis=0, keepdims=True)
    floor_middle = jnp.where(lane % H < pairs, floor_middle, 1.0)

    def whitened(m, low):
        scale = 1.0 / (mag_ref[m] + low)
        return jnp.concatenate([cross_ref[m, :B] * scale, cross_ref[m, B:] * scale], 0).astype(BF16)

    y_middle = dot(back_left[:B], whitened(pairs, floor_middle))
    y = dot(back_left, jnp.concatenate([whitened(m, floor[m : m + 1]) for m in range(pairs)], 1))
    is_zero = lane % H == 0
    both = []
    for m in range(pairs):
        turned = y_middle if m == 0 else pltpu.roll(y_middle, B - m, 1)
        imag = jnp.where(is_zero, turned, y[B:, m * B : m * B + B])
        both.append(jnp.concatenate([y[:B, m * B : m * B + B].astype(BF16), imag.astype(BF16)], 1))
    result = dot(jnp.concatenate(both, 0), back_right)
    sends = []
    for m in range(pairs):
        result_ref[2 * m] = result[m * B : m * B + B, :B]
        result_ref[2 * m + 1] = result[m * B : m * B + B, B:]
        sends.append(
            pltpu.make_async_copy(result_ref.at[pl.ds(2 * m, 2)], out.at[0, pl.ds(2 * (at + m), 2)], sems.at[m])
        )
        sends[-1].start()
    for send in sends:
        send.wait()


def correlate_early(cur_ref, a_ref, anchor_ref, *refs):
    is_first = lax.axis_index("sec") == 0
    blocks = [jnp.where(is_first, anchor_ref[m], a_ref[m]) for m in range(EARLY)]
    correlate_chunk(cur_ref, blocks, refs[:5], refs[5], 0, *refs[6:])


def correlate_late(held, cur_ref, a_ref, b_ref, rim_ref, anchor_ref, border_ref, *refs):
    del held
    is_first = lax.axis_index("sec") == 0
    blocks = [jnp.where(is_first, anchor_ref[EARLY - 1], a_ref[EARLY - 1])]
    blocks += [jnp.where(is_first, anchor_ref[EARLY + m], b_ref[m]) for m in range(b_ref.shape[0])]
    blocks += [unpacked_rim(jnp.where(is_first, border_ref[...], rim_ref[...]))]
    correlate_chunk(cur_ref, blocks, refs[:5], refs[5], EARLY - 1, *refs[6:])


SMEM = pl.BlockSpec(memory_space=pltpu.SMEM)
VMEM = pl.BlockSpec(memory_space=pltpu.VMEM)
ANY = pl.BlockSpec(memory_space=pl.ANY)
HBM = pl.BlockSpec(memory_space=pltpu.HBM)


def call(kernel, out_shape, in_specs, out_specs, scratch, flops, moved, args, aliases=None, grid=None, limit=VMEM_LIMIT):
    extra = {} if grid is None else {"grid": grid}
    return pl.pallas_call(
        kernel,
        out_shape=out_shape,
        in_specs=in_specs,
        out_specs=out_specs,
        scratch_shapes=scratch,
        input_output_aliases=aliases or {},
        compiler_params=pltpu.CompilerParams(vmem_limit_bytes=limit),
        cost_estimate=pl.CostEstimate(flops=flops, bytes_accessed=moved, transcendentals=0),
        **extra,
    )(*args)


def body(image, weight, lens_filter_taps, block_src, block_dst, valid_count, anchor):
    rows, cols = image.shape[1:]
    strips = lax.axis_size("tile")
    sections = lax.axis_size("sec")
    slots = block_src.shape[-1]
    count = anchor.shape[0]
    shape = jax.ShapeDtypeStruct
    whole = lambda *dims: pl.BlockSpec(dims, lambda i: (0,) * len(dims))
    back = [(i + 1, i) for i in range(strips - 1)]
    inner, outer = call(
        prepare_kernel,
        (shape((EDGE, cols), BF16), shape((2 * EDGE, cols), BF16)),
        [HBM],
        (VMEM,) * 2,
        [pltpu.SemaphoreType.DMA((2,))],
        2**33,
        2**17,
        (image,),
        limit=PREPARE_VMEM_LIMIT,
    )
    outer = lax.ppermute(outer, "tile", [(t, t + 2 * (t % 2) - 1) for t in range(1, strips - 1)])
    inner = lax.ppermute(inner, "tile", [(t, t ^ 1) for t in range(strips)])
    tile_blocks = rows // B * (cols // B)
    blocks, edge, bands = call(
        lens_kernel,
        (shape((tile_blocks, B, B), BF16), shape((2 * EDGE, cols), F32), shape((4 * EDGE, 10 * EDGE), BF16)),
        [SMEM, VMEM, VMEM],
        (VMEM, VMEM, VMEM),
        [],
        2**10,
        2**10,
        (lens_filter_taps, image, weight),
    )
    outgoing, places = call(
        pick_kernel,
        (shape((strips, slots, B, B), BF16), shape((1, strips, 1, slots), jnp.int32)),
        [VMEM, SMEM, SMEM] + [VMEM] * 6,
        (VMEM, VMEM),
        [pltpu.VMEM((tile_blocks, EDGE, B), BF16)],
        2**20,
        4 * 2 * rows * cols,
        (bands, block_src, valid_count, inner, outer, edge, weight, blocks, block_dst),
    )
    incoming = lax.all_to_all(outgoing, "tile", split_axis=0, concat_axis=0, tiled=True)
    part_a, rest = call(
        strip_kernel,
        (shape((EARLY, B, B), BF16), shape((count - EARLY, B, B), F32)),
        [SMEM, VMEM],
        (VMEM, VMEM),
        [pltpu.VMEM((count, B, B), F32)],
        2**20,
        4 * 2 * rows * cols,
        (places, incoming),
    )
    part_b, first, anchor_first = call(
        rest_kernel,
        (shape((count - EARLY, B, B), BF16), shape((H, B), BF16), shape((H, B), BF16)),
        [VMEM] * 3,
        (VMEM, VMEM, VMEM),
        [],
        2**18,
        6 * EARLY * B * B,
        (part_a, rest, anchor),
    )
    on = [(i, i + 1) for i in range(sections - 1)]
    prior_a = lax.ppermute(part_a, "sec", on)
    prior_b = lax.ppermute(part_b, "sec", on)
    own_rim = lax.ppermute(first, "tile", back)
    across = [(s * strips + d + 1, (s + 1) * strips + d) for s in range(sections - 1) for d in range(strips - 1)]
    prior_rim = lax.ppermute(first, ("sec", "tile"), across)
    border = lax.ppermute(anchor_first, "tile", back)
    right, left, middle, back_left, back_right = (jnp.asarray(t) for t in tables())
    early, late = EARLY - 1, count - EARLY + 1
    current = lambda kernel, pairs, *parts: call(
        kernel,
        shape((2 * B, (pairs + 1) * B), BF16),
        [VMEM] * (len(parts) + 3),
        VMEM,
        [],
        2**10,
        2**10,
        (*parts, right, left, middle),
    )
    spectra_a = current(early_kernel, early, part_a)
    spectra_b = current(late_kernel, late, part_a, part_b, own_rim)
    result = shape((1, 2 * count, B, B), F32)
    scratch = lambda pairs: [
        pltpu.VMEM((pairs + 1, 2 * B, B), F32),
        pltpu.VMEM((pairs + 1, B, B), F32),
        pltpu.VMEM((2 * pairs, B, B), F32),
        pltpu.SemaphoreType.DMA((pairs,)),
    ]
    held = call(
        correlate_early,
        result,
        [VMEM] * 8,
        HBM,
        scratch(early),
        2**10,
        2**10,
        (spectra_a, prior_a, anchor, right, left, middle, back_left, back_right),
    )
    return call(
        correlate_late,
        result,
        [HBM] + [VMEM] * 11,
        HBM,
        scratch(late),
        2**30,
        2**22,
        (held, spectra_b, prior_a, prior_b, prior_rim, anchor, border, right, left, middle, back_left, back_right),
        aliases={0: 0},
    )


def solution(mesh):
    in_specs = (
        P("sec", "tile", None),
        P("sec", "tile", None),
        P("sec", "tile", None),
        P("sec", "tile", None, None),
        P("sec", None, "tile", None),
        P("sec", "tile", None),
        P("tile", None, None),
    )
    out_specs = P("sec", "tile", None, None)
    return jax.shard_map(body, mesh=mesh, in_specs=in_specs, out_specs=out_specs, check_vma=False)
```

```python
import jax
import jax.numpy as jnp
import numpy as np
from jax import lax
from jax.experimental import pallas as pl
from jax.experimental.pallas import tpu as pltpu
from jax.sharding import PartitionSpec as P

B = 128
H = B // 2
EDGE = 16
EARLY = 11
PAIRS = 10
F32 = jnp.float32
BF16 = jnp.bfloat16
VMEM_LIMIT = 48 * 2**20
PREPARE_VMEM_LIMIT = 54912 * 2**10


def tables():
    j = np.arange(B)
    angle = (j[:, None] * j[None, :] % B) * (2.0 * np.pi / B)
    c, s = np.cos(angle), np.sin(angle)
    right = np.zeros((2 * B, 2 * B))
    for half, start in ((0, 0), (1, H)):
        right[start : start + B, half * H : half * H + H] = c[:, :H]
        right[start : start + B, B + half * H : B + half * H + H] = s[:, :H]
    left = np.block([[c, -s], [-s, -c]])
    q = np.arange((PAIRS + 1) * B)
    sign = 1.0 - 2.0 * (q % 2)
    middle = np.zeros(((PAIRS + 1) * B, B))
    for m in range(PAIRS):
        middle[:, m] = sign * (q // B == m)
        middle[:, H + m] = sign * ((q - H) // B == m)
    back_left = np.block([[c, -s], [s, c]])
    twice = np.where(j[:H] == 0, 1.0, 2.0)[:, None] / B
    back_right = np.zeros((2 * B, 2 * B))
    imag = -twice * s[:H]
    imag[0] = (1.0 - 2.0 * (j % 2)) / B
    for half in range(2):
        lanes = slice(half * B, half * B + B)
        back_right[half * H : half * H + H, lanes] = twice * c[:H]
        back_right[B + half * H : B + half * H + H, lanes] = imag
    return tuple(np.asarray(t, np.float32).astype(BF16) for t in (right, left, middle, back_left, back_right))


def dot(a, b):
    return jnp.dot(a, b, preferred_element_type=F32)


def shifted(x, off):
    rows = x.shape[0]
    if off == 0:
        return x
    gap = jnp.zeros((rows, abs(off)), x.dtype)
    if off > 0:
        return jnp.concatenate([x[:, off:], gap], 1)
    return jnp.concatenate([gap, x[:, :off]], 1)


def banded(taps_ref, which, valid):
    high, low = [], []
    for b in range(5):
        band = jnp.zeros(which.shape, F32)
        for a in range(5):
            tap = taps_ref[0, :, 5 * a + b : 5 * a + b + 1]
            band = jnp.where(which == a, tap, band)
        if valid is not None:
            band = jnp.where(valid, band, 0.0)
        top = band.astype(BF16)
        high.append(top)
        low.append((band - top.astype(F32)).astype(BF16))
    return jnp.concatenate([jnp.concatenate(high, 1), jnp.concatenate(low, 1)], 0)


def prepare_kernel(image, inner, outer, sems):
    last = image.shape[1] - EDGE
    odd = lax.rem(lax.axis_index("tile"), 2)
    to_inner = pltpu.make_async_copy(image.at[0, pl.ds(pl.multiple_of((1 - odd) * last, EDGE), EDGE)], inner, sems.at[0])
    wide = outer.shape[0]
    last = image.shape[1] - wide
    to_outer = pltpu.make_async_copy(image.at[0, pl.ds(pl.multiple_of(odd * last, EDGE), wide)], outer, sems.at[1])
    to_inner.start()
    to_outer.start()
    to_inner.wait()
    to_outer.wait()


def edge_bands(taps_ref):
    e = lax.broadcasted_iota(jnp.int32, (2 * EDGE, 2 * EDGE), 0)
    k = lax.broadcasted_iota(jnp.int32, (2 * EDGE, 2 * EDGE), 1)
    upper = (e < EDGE) & (k < EDGE)
    lower = (e >= EDGE) & (k >= EDGE)
    return banded(taps_ref, jnp.where(upper, k - (EDGE - 2) - e, k + (EDGE + 2) - e), upper | lower)


def lens_kernel(taps_ref, image_ref, weight_ref, blocks_ref, edge_ref, bands_ref):
    x = image_ref[0]
    rows, cols = x.shape
    across = cols // B
    i = lax.broadcasted_iota(jnp.int32, (B, B), 0)
    j = lax.broadcasted_iota(jnp.int32, (B, B), 1)
    bands = banded(taps_ref, j - i + 2, None)
    columns = [shifted(x, b - 2) for b in range(5)]
    stack = jnp.concatenate([jnp.concatenate([c[:B] for c in columns], 0), jnp.concatenate([c[B:] for c in columns], 0)], 1)
    both = dot(bands, stack)
    main = both[:B] + both[B:]
    edges = edge_bands(taps_ref)
    bands_ref[...] = edges
    both = dot(edges, jnp.concatenate([c[B - EDGE : B + EDGE] for c in columns], 0))
    middle = both[: 2 * EDGE] + both[2 * EDGE :]
    corrected = jnp.concatenate(
        [
            main[: B - EDGE, :cols],
            main[B - EDGE :, :cols] + middle[EDGE:],
            main[:EDGE, cols:] + middle[:EDGE],
            main[EDGE:, cols:],
        ],
        0,
    )
    edge_ref[:EDGE] = corrected[:EDGE]
    edge_ref[EDGE:] = corrected[rows - EDGE :]
    weighted = (corrected * weight_ref[0].astype(F32)).astype(BF16)
    for k in range(rows // B * across):
        r, c = k // across * B, k % across * B
        blocks_ref[k] = weighted[r : r + B, c : c + B]


def pick_kernel(
    bands_ref, src, counts, inner_ref, outer_ref, edge_ref, weight_ref, blocks_ref, dst_ref, out, dst_out, fixed_ref, src_ref, count_ref, sems
):
    loads = [pltpu.make_async_copy(src, src_ref, sems.at[0]), pltpu.make_async_copy(counts, count_ref, sems.at[1])]
    for load in loads:
        load.start()
    dst_out[...] = dst_ref[...]
    rows, cols = weight_ref.shape[1:]
    across = cols // B
    count = rows // B * across
    odd = lax.rem(lax.axis_index("tile"), 2) == 1
    inner, outer = inner_ref[...], outer_ref[...]
    rim = jnp.concatenate([jnp.where(odd, inner, outer[EDGE:]), jnp.where(odd, outer[:EDGE], inner)], 0)
    rims = jnp.concatenate([shifted(rim, b - 2) for b in range(5)], 0)
    both = dot(bands_ref[...], rims)
    corrected = edge_ref[...] + (both[: 2 * EDGE] + both[2 * EDGE :])
    top = (corrected[:EDGE] * weight_ref[0, :EDGE].astype(F32)).astype(BF16)
    bottom = (corrected[EDGE:] * weight_ref[0, rows - EDGE :].astype(F32)).astype(BF16)
    for c in range(across):
        fixed_ref[c] = top[:, c * B : c * B + B]
        fixed_ref[count - across + c] = bottom[:, c * B : c * B + B]
    for load in loads:
        load.wait()
    places = []
    for d in range(out.shape[0]):
        for q in range(out.shape[1]):
            live = q < count_ref[0, 0, d]
            block = src_ref[0, 0, d, q]
            out[d, q] = jnp.where(live, blocks_ref[block], jnp.zeros((), BF16))
            places.append((d, q, live, block))
    for d, q, live, block in places:
        at = pl.multiple_of(jnp.where(block < across, 0, B - EDGE), EDGE)
        out[d, q, pl.ds(at, EDGE), :] = jnp.where(live, fixed_ref[block], jnp.zeros((), BF16))


def strip_kernel(dst, in_ref, a_ref, rest_ref, acc_ref, dst_ref, sem):
    load = pltpu.make_async_copy(dst, dst_ref, sem)
    load.start()
    acc_ref[...] = jnp.zeros_like(acc_ref)
    load.wait()
    for d in range(in_ref.shape[0]):
        for q in range(in_ref.shape[1]):
            j = dst_ref[0, d, 0, q]
            acc_ref[j] = acc_ref[j] + in_ref[d, q].astype(F32)
    a_ref[...] = acc_ref[:EARLY].astype(BF16)
    rest_ref[...] = acc_ref[EARLY:]


def packed_rim(block):
    return jnp.concatenate([block[:H, :H], block[H:, :H]], 1)


def unpacked_rim(rim):
    gap = jnp.zeros((H, H), rim.dtype)
    return jnp.concatenate([jnp.concatenate([rim[:, :H], gap], 1), jnp.concatenate([rim[:, H:], gap], 1)], 0)


def rest_kernel(a_ref, rest_ref, anchor_ref, b_ref, first_ref, anchor_first_ref):
    b_ref[...] = rest_ref[...].astype(BF16)
    first_ref[...] = packed_rim(a_ref[0])
    anchor_first_ref[...] = packed_rim(anchor_ref[0])


def forward(blocks, right, left, middle):
    pairs = len(blocks) - 1
    both = jnp.concatenate([jnp.concatenate([blocks[m], blocks[m + 1]], 1) for m in range(pairs)], 0)
    p = dot(both, right).astype(BF16)
    re = [p[m * B : m * B + B, :B] for m in range(pairs)]
    im = [p[m * B : m * B + B, B:] for m in range(pairs)]
    spectra = dot(left, jnp.concatenate([jnp.concatenate(re, 1), jnp.concatenate(im, 1)], 0))
    p = dot(jnp.concatenate(blocks, 1), middle[: (pairs + 1) * B]).astype(BF16)
    return spectra, dot(left[:, :B], p)


def spectra_out(blocks, right_ref, left_ref, middle_ref, out_ref):
    spectra, rest = forward(blocks, right_ref[...], left_ref[...], middle_ref[...])
    out_ref[:, : spectra.shape[1]] = spectra.astype(BF16)
    out_ref[:, spectra.shape[1] :] = rest.astype(BF16)


def early_kernel(a_ref, *refs):
    spectra_out([a_ref[m] for m in range(EARLY)], *refs)


def late_kernel(a_ref, b_ref, rim_ref, *refs):
    spectra_out([a_ref[EARLY - 1]] + [b_ref[m] for m in range(b_ref.shape[0])] + [unpacked_rim(rim_ref[...])], *refs)


def correlate_chunk(cur_ref, blocks, tables, out, at, cross_ref, mag_ref, result_ref, sems):
    right, left, middle, back_left, back_right = (table[...] for table in tables)
    pairs = len(blocks) - 1
    lane = lax.broadcasted_iota(jnp.int32, (1, B), 1)
    twice = jnp.where(lane % H == 0, 1.0, 2.0)
    sums = []
    spectra, rest = forward(blocks, right, left, middle)
    for m in range(pairs + 1):
        f = spectra[:, m * B : m * B + B] if m < pairs else rest
        c = cur_ref[:, m * B : m * B + B].astype(F32)
        ar, ai, br, bi = c[:B], c[B:], f[:B], f[B:]
        re = ar * br + ai * bi
        im = ai * br - ar * bi
        square = re * re + im * im
        mag = square * lax.rsqrt(jnp.maximum(square, 1e-30))
        cross_ref[m, :B] = re
        cross_ref[m, B:] = im
        mag_ref[m] = mag
        total = jnp.sum(mag, axis=0, keepdims=True)
        sums.append(total * twice if m < pairs else total)
    row = lax.broadcasted_iota(jnp.int32, (pairs, B), 0)
    lanes = lax.broadcasted_iota(jnp.int32, (pairs, B), 1)
    mine = row == lanes % H
    table = jnp.concatenate(sums[:pairs], 0) + jnp.where(mine, sums[pairs], 0.0)
    aligned = lanes < H
    first = jnp.sum(jnp.where(aligned, table, 0.0), axis=1, keepdims=True)
    second = jnp.sum(jnp.where(aligned, 0.0, table), axis=1, keepdims=True)
    floor = jnp.where(aligned, first, second) * (0.1 / (B * B)) + 1e-6
    floor_middle = jnp.sum(jnp.where(mine, floor, 0.0), axis=0, keepdims=True)
    floor_middle = jnp.where(lane % H < pairs, floor_middle, 1.0)

    def whitened(m, low):
        scale = 1.0 / (mag_ref[m] + low)
        return jnp.concatenate([cross_ref[m, :B] * scale, cross_ref[m, B:] * scale], 0).astype(BF16)

    y_middle = dot(back_left[:B], whitened(pairs, floor_middle))
    y = dot(back_left, jnp.concatenate([whitened(m, floor[m : m + 1]) for m in range(pairs)], 1))
    is_zero = lane % H == 0
    both = []
    for m in range(pairs):
        turned = y_middle if m == 0 else pltpu.roll(y_middle, B - m, 1)
        imag = jnp.where(is_zero, turned, y[B:, m * B : m * B + B])
        both.append(jnp.concatenate([y[:B, m * B : m * B + B].astype(BF16), imag.astype(BF16)], 1))
    result = dot(jnp.concatenate(both, 0), back_right)
    sends = []
    for m in range(pairs):
        result_ref[2 * m] = result[m * B : m * B + B, :B]
        result_ref[2 * m + 1] = result[m * B : m * B + B, B:]
        sends.append(
            pltpu.make_async_copy(result_ref.at[pl.ds(2 * m, 2)], out.at[0, pl.ds(2 * (at + m), 2)], sems.at[m])
        )
        sends[-1].start()
    for send in sends:
        send.wait()


def correlate_early(cur_ref, a_ref, anchor_ref, *refs):
    is_first = lax.axis_index("sec") == 0
    blocks = [jnp.where(is_first, anchor_ref[m], a_ref[m]) for m in range(EARLY)]
    correlate_chunk(cur_ref, blocks, refs[:5], refs[5], 0, *refs[6:])


def correlate_late(held, cur_ref, a_ref, b_ref, rim_ref, anchor_ref, border_ref, *refs):
    del held
    is_first = lax.axis_index("sec") == 0
    blocks = [jnp.where(is_first, anchor_ref[EARLY - 1], a_ref[EARLY - 1])]
    blocks += [jnp.where(is_first, anchor_ref[EARLY + m], b_ref[m]) for m in range(b_ref.shape[0])]
    blocks += [unpacked_rim(jnp.where(is_first, border_ref[...], rim_ref[...]))]
    correlate_chunk(cur_ref, blocks, refs[:5], refs[5], EARLY - 1, *refs[6:])


SMEM = pl.BlockSpec(memory_space=pltpu.SMEM)
VMEM = pl.BlockSpec(memory_space=pltpu.VMEM)
ANY = pl.BlockSpec(memory_space=pl.ANY)
HBM = pl.BlockSpec(memory_space=pltpu.HBM)


def call(kernel, out_shape, in_specs, out_specs, scratch, flops, moved, args, aliases=None, grid=None, limit=VMEM_LIMIT):
    extra = {} if grid is None else {"grid": grid}
    return pl.pallas_call(
        kernel,
        out_shape=out_shape,
        in_specs=in_specs,
        out_specs=out_specs,
        scratch_shapes=scratch,
        input_output_aliases=aliases or {},
        compiler_params=pltpu.CompilerParams(vmem_limit_bytes=limit),
        cost_estimate=pl.CostEstimate(flops=flops, bytes_accessed=moved, transcendentals=0),
        **extra,
    )(*args)


def body(image, weight, lens_filter_taps, block_src, block_dst, valid_count, anchor):
    rows, cols = image.shape[1:]
    strips = lax.axis_size("tile")
    sections = lax.axis_size("sec")
    slots = block_src.shape[-1]
    count = anchor.shape[0]
    shape = jax.ShapeDtypeStruct
    whole = lambda *dims: pl.BlockSpec(dims, lambda i: (0,) * len(dims))
    back = [(i + 1, i) for i in range(strips - 1)]
    inner, outer = call(
        prepare_kernel,
        (shape((EDGE, cols), BF16), shape((2 * EDGE, cols), BF16)),
        [HBM],
        (VMEM,) * 2,
        [pltpu.SemaphoreType.DMA((2,))],
        2**33,
        2**17,
        (image,),
        limit=PREPARE_VMEM_LIMIT,
    )
    outer = lax.ppermute(outer, "tile", [(t, t + 2 * (t % 2) - 1) for t in range(1, strips - 1)])
    inner = lax.ppermute(inner, "tile", [(t, t ^ 1) for t in range(strips)])
    tile_blocks = rows // B * (cols // B)
    blocks, edge, bands = call(
        lens_kernel,
        (shape((tile_blocks, B, B), BF16), shape((2 * EDGE, cols), F32), shape((4 * EDGE, 10 * EDGE), BF16)),
        [VMEM, VMEM, VMEM],
        (VMEM, VMEM, VMEM),
        [],
        2**10,
        2**10,
        (lens_filter_taps, image, weight),
    )
    outgoing, places = call(
        pick_kernel,
        (shape((strips, slots, B, B), BF16), shape((1, strips, 1, slots), jnp.int32)),
        [VMEM] * 9,
        (VMEM, VMEM),
        [
            pltpu.VMEM((tile_blocks, EDGE, B), BF16),
            pltpu.SMEM(block_src.shape, jnp.int32),
            pltpu.SMEM(valid_count.shape, jnp.int32),
            pltpu.SemaphoreType.DMA((2,)),
        ],
        2**20,
        4 * 2 * rows * cols,
        (bands, block_src, valid_count, inner, outer, edge, weight, blocks, block_dst),
    )
    incoming = lax.all_to_all(outgoing, "tile", split_axis=0, concat_axis=0, tiled=True)
    part_a, rest = call(
        strip_kernel,
        (shape((EARLY, B, B), BF16), shape((count - EARLY, B, B), F32)),
        [VMEM, VMEM],
        (VMEM, VMEM),
        [pltpu.VMEM((count, B, B), F32), pltpu.SMEM(block_dst.shape, jnp.int32), pltpu.SemaphoreType.DMA],
        2**20,
        4 * 2 * rows * cols,
        (places, incoming),
    )
    part_b, first, anchor_first = call(
        rest_kernel,
        (shape((count - EARLY, B, B), BF16), shape((H, B), BF16), shape((H, B), BF16)),
        [VMEM] * 3,
        (VMEM, VMEM, VMEM),
        [],
        2**18,
        6 * EARLY * B * B,
        (part_a, rest, anchor),
    )
    on = [(i, i + 1) for i in range(sections - 1)]
    prior_a = lax.ppermute(part_a, "sec", on)
    prior_b = lax.ppermute(part_b, "sec", on)
    own_rim = lax.ppermute(first, "tile", back)
    across = [(s * strips + d + 1, (s + 1) * strips + d) for s in range(sections - 1) for d in range(strips - 1)]
    prior_rim = lax.ppermute(first, ("sec", "tile"), across)
    border = lax.ppermute(anchor_first, "tile", back)
    right, left, middle, back_left, back_right = (jnp.asarray(t) for t in tables())
    early, late = EARLY - 1, count - EARLY + 1
    current = lambda kernel, pairs, *parts: call(
        kernel,
        shape((2 * B, (pairs + 1) * B), BF16),
        [VMEM] * (len(parts) + 3),
        VMEM,
        [],
        2**10,
        2**10,
        (*parts, right, left, middle),
    )
    spectra_a = current(early_kernel, early, part_a)
    spectra_b = current(late_kernel, late, part_a, part_b, own_rim)
    result = shape((1, 2 * count, B, B), F32)
    scratch = lambda pairs: [
        pltpu.VMEM((pairs + 1, 2 * B, B), F32),
        pltpu.VMEM((pairs + 1, B, B), F32),
        pltpu.VMEM((2 * pairs, B, B), F32),
        pltpu.SemaphoreType.DMA((pairs,)),
    ]
    held = call(
        correlate_early,
        result,
        [VMEM] * 8,
        HBM,
        scratch(early),
        2**10,
        2**10,
        (spectra_a, prior_a, anchor, right, left, middle, back_left, back_right),
    )
    return call(
        correlate_late,
        result,
        [HBM] + [VMEM] * 11,
        HBM,
        scratch(late),
        2**30,
        2**22,
        (held, spectra_b, prior_a, prior_b, prior_rim, anchor, border, right, left, middle, back_left, back_right),
        aliases={0: 0},
    )


def solution(mesh):
    in_specs = (
        P("sec", "tile", None),
        P("sec", "tile", None),
        P("sec", "tile", None),
        P("sec", "tile", None, None),
        P("sec", None, "tile", None),
        P("sec", "tile", None),
        P("tile", None, None),
    )
    out_specs = P("sec", "tile", None, None)
    return jax.shard_map(body, mesh=mesh, in_specs=in_specs, out_specs=out_specs, check_vma=False)
```

```python
import jax
import jax.numpy as jnp
import numpy as np
from jax import lax
from jax.experimental import pallas as pl
from jax.experimental.pallas import tpu as pltpu
from jax.sharding import PartitionSpec as P

B = 128
H = B // 2
EDGE = 16
EARLY = 11
PAIRS = 10
F32 = jnp.float32
BF16 = jnp.bfloat16
VMEM_LIMIT = 48 * 2**20
PREPARE_VMEM_LIMIT = 54912 * 2**10


def tables():
    j = np.arange(B)
    angle = (j[:, None] * j[None, :] % B) * (2.0 * np.pi / B)
    c, s = np.cos(angle), np.sin(angle)
    right = np.zeros((2 * B, 2 * B))
    for half, start in ((0, 0), (1, H)):
        right[start : start + B, half * H : half * H + H] = c[:, :H]
        right[start : start + B, B + half * H : B + half * H + H] = s[:, :H]
    left = np.block([[c, -s], [-s, -c]])
    q = np.arange((PAIRS + 1) * B)
    sign = 1.0 - 2.0 * (q % 2)
    middle = np.zeros(((PAIRS + 1) * B, B))
    for m in range(PAIRS):
        middle[:, m] = sign * (q // B == m)
        middle[:, H + m] = sign * ((q - H) // B == m)
    back_left = np.block([[c, -s], [s, c]])
    twice = np.where(j[:H] == 0, 1.0, 2.0)[:, None] / B
    back_right = np.zeros((2 * B, 2 * B))
    imag = -twice * s[:H]
    imag[0] = (1.0 - 2.0 * (j % 2)) / B
    for half in range(2):
        lanes = slice(half * B, half * B + B)
        back_right[half * H : half * H + H, lanes] = twice * c[:H]
        back_right[B + half * H : B + half * H + H, lanes] = imag
    return tuple(np.asarray(t, np.float32).astype(BF16) for t in (right, left, middle, back_left, back_right))


def dot(a, b):
    return jnp.dot(a, b, preferred_element_type=F32)


def shifted(x, off):
    rows = x.shape[0]
    if off == 0:
        return x
    gap = jnp.zeros((rows, abs(off)), x.dtype)
    if off > 0:
        return jnp.concatenate([x[:, off:], gap], 1)
    return jnp.concatenate([gap, x[:, :off]], 1)


def banded(taps_ref, which, valid):
    high, low = [], []
    for b in range(5):
        band = jnp.zeros(which.shape, F32)
        for a in range(5):
            tap = taps_ref[0, :, 5 * a + b : 5 * a + b + 1]
            band = jnp.where(which == a, tap, band)
        if valid is not None:
            band = jnp.where(valid, band, 0.0)
        top = band.astype(BF16)
        high.append(top)
        low.append((band - top.astype(F32)).astype(BF16))
    return jnp.concatenate([jnp.concatenate(high, 1), jnp.concatenate(low, 1)], 0)


def prepare_kernel(image, inner, outer, sems):
    last = image.shape[1] - EDGE
    odd = lax.rem(lax.axis_index("tile"), 2)
    to_inner = pltpu.make_async_copy(image.at[0, pl.ds(pl.multiple_of((1 - odd) * last, EDGE), EDGE)], inner, sems.at[0])
    wide = outer.shape[0]
    last = image.shape[1] - wide
    to_outer = pltpu.make_async_copy(image.at[0, pl.ds(pl.multiple_of(odd * last, EDGE), wide)], outer, sems.at[1])
    to_inner.start()
    to_outer.start()
    to_inner.wait()
    to_outer.wait()


def edge_bands(taps_ref):
    e = lax.broadcasted_iota(jnp.int32, (2 * EDGE, 2 * EDGE), 0)
    k = lax.broadcasted_iota(jnp.int32, (2 * EDGE, 2 * EDGE), 1)
    upper = (e < EDGE) & (k < EDGE)
    lower = (e >= EDGE) & (k >= EDGE)
    return banded(taps_ref, jnp.where(upper, k - (EDGE - 2) - e, k + (EDGE + 2) - e), upper | lower)


def lens_kernel(taps_ref, image_ref, weight_ref, blocks_ref, edge_ref, bands_ref):
    x = image_ref[0]
    rows, cols = x.shape
    across = cols // B
    i = lax.broadcasted_iota(jnp.int32, (B, B), 0)
    j = lax.broadcasted_iota(jnp.int32, (B, B), 1)
    bands = banded(taps_ref, j - i + 2, None)
    columns = [shifted(x, b - 2) for b in range(5)]
    stack = jnp.concatenate([jnp.concatenate([c[:B] for c in columns], 0), jnp.concatenate([c[B:] for c in columns], 0)], 1)
    both = dot(bands, stack)
    main = both[:B] + both[B:]
    edges = edge_bands(taps_ref)
    bands_ref[...] = edges
    both = dot(edges, jnp.concatenate([c[B - EDGE : B + EDGE] for c in columns], 0))
    middle = both[: 2 * EDGE] + both[2 * EDGE :]
    corrected = jnp.concatenate(
        [
            main[: B - EDGE, :cols],
            main[B - EDGE :, :cols] + middle[EDGE:],
            main[:EDGE, cols:] + middle[:EDGE],
            main[EDGE:, cols:],
        ],
        0,
    )
    edge_ref[:EDGE] = corrected[:EDGE]
    edge_ref[EDGE:] = corrected[rows - EDGE :]
    weighted = (corrected * weight_ref[0].astype(F32)).astype(BF16)
    for k in range(rows // B * across):
        r, c = k // across * B, k % across * B
        blocks_ref[k] = weighted[r : r + B, c : c + B]


def pick_kernel(
    bands_ref, src, counts, inner_ref, outer_ref, edge_ref, weight_ref, blocks_ref, dst_ref, out, dst_out, fixed_ref, src_ref, count_ref, sems
):
    loads = [pltpu.make_async_copy(src, src_ref, sems.at[0]), pltpu.make_async_copy(counts, count_ref, sems.at[1])]
    for load in loads:
        load.start()
    dst_out[...] = dst_ref[...]
    rows, cols = weight_ref.shape[1:]
    across = cols // B
    count = rows // B * across
    odd = lax.rem(lax.axis_index("tile"), 2) == 1
    inner, outer = inner_ref[...], outer_ref[...]
    rim = jnp.concatenate([jnp.where(odd, inner, outer[EDGE:]), jnp.where(odd, outer[:EDGE], inner)], 0)
    rims = jnp.concatenate([shifted(rim, b - 2) for b in range(5)], 0)
    both = dot(bands_ref[...], rims)
    for load in loads:
        load.wait()
    places = []
    for d in range(out.shape[0]):
        for q in range(out.shape[1]):
            live = q < count_ref[0, 0, d]
            block = src_ref[0, 0, q, d]
            out[d, q] = jnp.where(live, blocks_ref[block], jnp.zeros((), BF16))
            places.append((d, q, live, block))
    corrected = edge_ref[...] + (both[: 2 * EDGE] + both[2 * EDGE :])
    top = (corrected[:EDGE] * weight_ref[0, :EDGE].astype(F32)).astype(BF16)
    bottom = (corrected[EDGE:] * weight_ref[0, rows - EDGE :].astype(F32)).astype(BF16)
    for c in range(across):
        fixed_ref[c] = top[:, c * B : c * B + B]
        fixed_ref[count - across + c] = bottom[:, c * B : c * B + B]
    for d, q, live, block in places:
        at = pl.multiple_of(jnp.where(block < across, 0, B - EDGE), EDGE)
        out[d, q, pl.ds(at, EDGE), :] = jnp.where(live, fixed_ref[block], jnp.zeros((), BF16))


def strip_kernel(dst, in_ref, a_ref, rest_ref, acc_ref, dst_ref, sem):
    load = pltpu.make_async_copy(dst, dst_ref, sem)
    load.start()
    acc_ref[...] = jnp.zeros_like(acc_ref)
    load.wait()
    for d in range(in_ref.shape[0]):
        for q in range(in_ref.shape[1]):
            j = dst_ref[0, 0, q, d]
            acc_ref[j] = acc_ref[j] + in_ref[d, q].astype(F32)
    a_ref[...] = acc_ref[:EARLY].astype(BF16)
    rest_ref[...] = acc_ref[EARLY:]


def packed_rim(block):
    return jnp.concatenate([block[:H, :H], block[H:, :H]], 1)


def unpacked_rim(rim):
    gap = jnp.zeros((H, H), rim.dtype)
    return jnp.concatenate([jnp.concatenate([rim[:, :H], gap], 1), jnp.concatenate([rim[:, H:], gap], 1)], 0)


def rest_kernel(a_ref, rest_ref, anchor_ref, b_ref, first_ref, anchor_first_ref):
    b_ref[...] = rest_ref[...].astype(BF16)
    first_ref[...] = packed_rim(a_ref[0])
    anchor_first_ref[...] = packed_rim(anchor_ref[0])


def forward(blocks, right, left, middle):
    pairs = len(blocks) - 1
    both = jnp.concatenate([jnp.concatenate([blocks[m], blocks[m + 1]], 1) for m in range(pairs)], 0)
    p = dot(both, right).astype(BF16)
    re = [p[m * B : m * B + B, :B] for m in range(pairs)]
    im = [p[m * B : m * B + B, B:] for m in range(pairs)]
    spectra = dot(left, jnp.concatenate([jnp.concatenate(re, 1), jnp.concatenate(im, 1)], 0))
    p = dot(jnp.concatenate(blocks, 1), middle[: (pairs + 1) * B]).astype(BF16)
    return spectra, dot(left[:, :B], p)


def spectra_out(blocks, right_ref, left_ref, middle_ref, out_ref):
    spectra, rest = forward(blocks, right_ref[...], left_ref[...], middle_ref[...])
    out_ref[:, : spectra.shape[1]] = spectra.astype(BF16)
    out_ref[:, spectra.shape[1] :] = rest.astype(BF16)


def early_kernel(a_ref, *refs):
    spectra_out([a_ref[m] for m in range(EARLY)], *refs)


def late_kernel(a_ref, b_ref, rim_ref, *refs):
    spectra_out([a_ref[EARLY - 1]] + [b_ref[m] for m in range(b_ref.shape[0])] + [unpacked_rim(rim_ref[...])], *refs)


def correlate_chunk(cur_ref, blocks, tables, out, at, cross_ref, mag_ref, result_ref, sems):
    right, left, middle, back_left, back_right = (table[...] for table in tables)
    pairs = len(blocks) - 1
    lane = lax.broadcasted_iota(jnp.int32, (1, B), 1)
    twice = jnp.where(lane % H == 0, 1.0, 2.0)
    sums = []
    spectra, rest = forward(blocks, right, left, middle)
    for m in range(pairs + 1):
        f = spectra[:, m * B : m * B + B] if m < pairs else rest
        c = cur_ref[:, m * B : m * B + B].astype(F32)
        ar, ai, br, bi = c[:B], c[B:], f[:B], f[B:]
        re = ar * br + ai * bi
        im = ai * br - ar * bi
        square = re * re + im * im
        mag = square * lax.rsqrt(jnp.maximum(square, 1e-30))
        cross_ref[m, :B] = re
        cross_ref[m, B:] = im
        mag_ref[m] = mag
        total = jnp.sum(mag, axis=0, keepdims=True)
        sums.append(total * twice if m < pairs else total)
    row = lax.broadcasted_iota(jnp.int32, (pairs, B), 0)
    lanes = lax.broadcasted_iota(jnp.int32, (pairs, B), 1)
    mine = row == lanes % H
    table = jnp.concatenate(sums[:pairs], 0) + jnp.where(mine, sums[pairs], 0.0)
    aligned = lanes < H
    first = jnp.sum(jnp.where(aligned, table, 0.0), axis=1, keepdims=True)
    second = jnp.sum(jnp.where(aligned, 0.0, table), axis=1, keepdims=True)
    floor = jnp.where(aligned, first, second) * (0.1 / (B * B)) + 1e-6
    floor_middle = jnp.sum(jnp.where(mine, floor, 0.0), axis=0, keepdims=True)
    floor_middle = jnp.where(lane % H < pairs, floor_middle, 1.0)

    def whitened(m, low):
        scale = 1.0 / (mag_ref[m] + low)
        return jnp.concatenate([cross_ref[m, :B] * scale, cross_ref[m, B:] * scale], 0).astype(BF16)

    y_middle = dot(back_left[:B], whitened(pairs, floor_middle))
    y = dot(back_left, jnp.concatenate([whitened(m, floor[m : m + 1]) for m in range(pairs)], 1))
    is_zero = lane % H == 0
    both = []
    for m in range(pairs):
        turned = y_middle if m == 0 else pltpu.roll(y_middle, B - m, 1)
        imag = jnp.where(is_zero, turned, y[B:, m * B : m * B + B])
        both.append(jnp.concatenate([y[:B, m * B : m * B + B].astype(BF16), imag.astype(BF16)], 1))
    result = dot(jnp.concatenate(both, 0), back_right)
    sends = []
    for m in range(pairs):
        result_ref[2 * m] = result[m * B : m * B + B, :B]
        result_ref[2 * m + 1] = result[m * B : m * B + B, B:]
        sends.append(
            pltpu.make_async_copy(result_ref.at[pl.ds(2 * m, 2)], out.at[0, pl.ds(2 * (at + m), 2)], sems.at[m])
        )
        sends[-1].start()
    for send in sends:
        send.wait()


def correlate_early(cur_ref, a_ref, anchor_ref, *refs):
    is_first = lax.axis_index("sec") == 0
    blocks = [jnp.where(is_first, anchor_ref[m], a_ref[m]) for m in range(EARLY)]
    correlate_chunk(cur_ref, blocks, refs[:5], refs[5], 0, *refs[6:])


def correlate_late(held, cur_ref, a_ref, b_ref, rim_ref, anchor_ref, border_ref, *refs):
    del held
    is_first = lax.axis_index("sec") == 0
    blocks = [jnp.where(is_first, anchor_ref[EARLY - 1], a_ref[EARLY - 1])]
    blocks += [jnp.where(is_first, anchor_ref[EARLY + m], b_ref[m]) for m in range(b_ref.shape[0])]
    blocks += [unpacked_rim(jnp.where(is_first, border_ref[...], rim_ref[...]))]
    correlate_chunk(cur_ref, blocks, refs[:5], refs[5], EARLY - 1, *refs[6:])


SMEM = pl.BlockSpec(memory_space=pltpu.SMEM)
VMEM = pl.BlockSpec(memory_space=pltpu.VMEM)
ANY = pl.BlockSpec(memory_space=pl.ANY)
HBM = pl.BlockSpec(memory_space=pltpu.HBM)


def call(kernel, out_shape, in_specs, out_specs, scratch, flops, moved, args, aliases=None, grid=None, limit=VMEM_LIMIT):
    extra = {} if grid is None else {"grid": grid}
    return pl.pallas_call(
        kernel,
        out_shape=out_shape,
        in_specs=in_specs,
        out_specs=out_specs,
        scratch_shapes=scratch,
        input_output_aliases=aliases or {},
        compiler_params=pltpu.CompilerParams(vmem_limit_bytes=limit),
        cost_estimate=pl.CostEstimate(flops=flops, bytes_accessed=moved, transcendentals=0),
        **extra,
    )(*args)


def body(image, weight, lens_filter_taps, block_src, block_dst, valid_count, anchor):
    rows, cols = image.shape[1:]
    strips = lax.axis_size("tile")
    sections = lax.axis_size("sec")
    slots = block_src.shape[-1]
    count = anchor.shape[0]
    shape = jax.ShapeDtypeStruct
    block_src = block_src.transpose(0, 1, 3, 2)
    block_dst = block_dst.transpose(0, 2, 3, 1)
    whole = lambda *dims: pl.BlockSpec(dims, lambda i: (0,) * len(dims))
    back = [(i + 1, i) for i in range(strips - 1)]
    inner, outer = call(
        prepare_kernel,
        (shape((EDGE, cols), BF16), shape((2 * EDGE, cols), BF16)),
        [HBM],
        (VMEM,) * 2,
        [pltpu.SemaphoreType.DMA((2,))],
        2**33,
        2**17,
        (image,),
        limit=PREPARE_VMEM_LIMIT,
    )
    outer = lax.ppermute(outer, "tile", [(t, t + 2 * (t % 2) - 1) for t in range(1, strips - 1)])
    inner = lax.ppermute(inner, "tile", [(t, t ^ 1) for t in range(strips)])
    tile_blocks = rows // B * (cols // B)
    blocks, edge, bands = call(
        lens_kernel,
        (shape((tile_blocks, B, B), BF16), shape((2 * EDGE, cols), F32), shape((4 * EDGE, 10 * EDGE), BF16)),
        [VMEM, VMEM, VMEM],
        (VMEM, VMEM, VMEM),
        [],
        2**10,
        2**10,
        (lens_filter_taps, image, weight),
    )
    outgoing, places = call(
        pick_kernel,
        (shape((strips, slots, B, B), BF16), shape(block_dst.shape, jnp.int32)),
        [VMEM] * 9,
        (VMEM, VMEM),
        [
            pltpu.VMEM((tile_blocks, EDGE, B), BF16),
            pltpu.SMEM(block_src.shape, jnp.int32),
            pltpu.SMEM(valid_count.shape, jnp.int32),
            pltpu.SemaphoreType.DMA((2,)),
        ],
        2**20,
        4 * 2 * rows * cols,
        (bands, block_src, valid_count, inner, outer, edge, weight, blocks, block_dst),
    )
    incoming = lax.all_to_all(outgoing, "tile", split_axis=0, concat_axis=0, tiled=True)
    part_a, rest = call(
        strip_kernel,
        (shape((EARLY, B, B), BF16), shape((count - EARLY, B, B), F32)),
        [VMEM, VMEM],
        (VMEM, VMEM),
        [pltpu.VMEM((count, B, B), F32), pltpu.SMEM(block_dst.shape, jnp.int32), pltpu.SemaphoreType.DMA],
        2**20,
        4 * 2 * rows * cols,
        (places, incoming),
    )
    part_b, first, anchor_first = call(
        rest_kernel,
        (shape((count - EARLY, B, B), BF16), shape((H, B), BF16), shape((H, B), BF16)),
        [VMEM] * 3,
        (VMEM, VMEM, VMEM),
        [],
        2**18,
        6 * EARLY * B * B,
        (part_a, rest, anchor),
    )
    on = [(i, i + 1) for i in range(sections - 1)]
    prior_a = lax.ppermute(part_a, "sec", on)
    prior_b = lax.ppermute(part_b, "sec", on)
    own_rim = lax.ppermute(first, "tile", back)
    across = [(s * strips + d + 1, (s + 1) * strips + d) for s in range(sections - 1) for d in range(strips - 1)]
    prior_rim = lax.ppermute(first, ("sec", "tile"), across)
    border = lax.ppermute(anchor_first, "tile", back)
    right, left, middle, back_left, back_right = (jnp.asarray(t) for t in tables())
    early, late = EARLY - 1, count - EARLY + 1
    current = lambda kernel, pairs, *parts: call(
        kernel,
        shape((2 * B, (pairs + 1) * B), BF16),
        [VMEM] * (len(parts) + 3),
        VMEM,
        [],
        2**10,
        2**10,
        (*parts, right, left, middle),
    )
    spectra_a = current(early_kernel, early, part_a)
    spectra_b = current(late_kernel, late, part_a, part_b, own_rim)
    result = shape((1, 2 * count, B, B), F32)
    scratch = lambda pairs: [
        pltpu.VMEM((pairs + 1, 2 * B, B), F32),
        pltpu.VMEM((pairs + 1, B, B), F32),
        pltpu.VMEM((2 * pairs, B, B), F32),
        pltpu.SemaphoreType.DMA((pairs,)),
    ]
    held = call(
        correlate_early,
        result,
        [VMEM] * 8,
        HBM,
        scratch(early),
        2**10,
        2**10,
        (spectra_a, prior_a, anchor, right, left, middle, back_left, back_right),
    )
    return call(
        correlate_late,
        result,
        [HBM] + [VMEM] * 11,
        HBM,
        scratch(late),
        2**30,
        2**22,
        (held, spectra_b, prior_a, prior_b, prior_rim, anchor, border, right, left, middle, back_left, back_right),
        aliases={0: 0},
    )


def solution(mesh):
    in_specs = (
        P("sec", "tile", None),
        P("sec", "tile", None),
        P("sec", "tile", None),
        P("sec", "tile", None, None),
        P("sec", None, "tile", None),
        P("sec", "tile", None),
        P("tile", None, None),
    )
    out_specs = P("sec", "tile", None, None)
    return jax.shard_map(body, mesh=mesh, in_specs=in_specs, out_specs=out_specs, check_vma=False)
```

```python
import jax
import jax.numpy as jnp
import numpy as np
from jax import lax
from jax.experimental import pallas as pl
from jax.experimental.pallas import tpu as pltpu
from jax.sharding import PartitionSpec as P

B = 128
H = B // 2
EDGE = 16
EARLY = 11
PAIRS = 10
F32 = jnp.float32
BF16 = jnp.bfloat16
VMEM_LIMIT = 48 * 2**20
PREPARE_VMEM_LIMIT = 54912 * 2**10


def tables():
    j = np.arange(B)
    angle = (j[:, None] * j[None, :] % B) * (2.0 * np.pi / B)
    c, s = np.cos(angle), np.sin(angle)
    right = np.zeros((2 * B, 2 * B))
    for half, start in ((0, 0), (1, H)):
        right[start : start + B, half * H : half * H + H] = c[:, :H]
        right[start : start + B, B + half * H : B + half * H + H] = s[:, :H]
    left = np.block([[c, -s], [-s, -c]])
    q = np.arange((PAIRS + 1) * B)
    sign = 1.0 - 2.0 * (q % 2)
    middle = np.zeros(((PAIRS + 1) * B, B))
    for m in range(PAIRS):
        middle[:, m] = sign * (q // B == m)
        middle[:, H + m] = sign * ((q - H) // B == m)
    back_left = np.block([[c, -s], [s, c]])
    twice = np.where(j[:H] == 0, 1.0, 2.0)[:, None] / B
    back_right = np.zeros((2 * B, 2 * B))
    imag = -twice * s[:H]
    imag[0] = (1.0 - 2.0 * (j % 2)) / B
    for half in range(2):
        lanes = slice(half * B, half * B + B)
        back_right[half * H : half * H + H, lanes] = twice * c[:H]
        back_right[B + half * H : B + half * H + H, lanes] = imag
    return tuple(np.asarray(t, np.float32).astype(BF16) for t in (right, left, middle, back_left, back_right))


def dot(a, b):
    return jnp.dot(a, b, preferred_element_type=F32)


def shifted(x, off):
    rows = x.shape[0]
    if off == 0:
        return x
    gap = jnp.zeros((rows, abs(off)), x.dtype)
    if off > 0:
        return jnp.concatenate([x[:, off:], gap], 1)
    return jnp.concatenate([gap, x[:, :off]], 1)


def banded(taps_ref, which, valid):
    high, low = [], []
    for b in range(5):
        band = jnp.zeros(which.shape, F32)
        for a in range(5):
            tap = taps_ref[0, :, 5 * a + b : 5 * a + b + 1]
            band = jnp.where(which == a, tap, band)
        if valid is not None:
            band = jnp.where(valid, band, 0.0)
        top = band.astype(BF16)
        high.append(top)
        low.append((band - top.astype(F32)).astype(BF16))
    return jnp.concatenate([jnp.concatenate(high, 1), jnp.concatenate(low, 1)], 0)


def prepare_kernel(image, inner, outer, sems):
    last = image.shape[1] - EDGE
    odd = lax.rem(lax.axis_index("tile"), 2)
    to_inner = pltpu.make_async_copy(image.at[0, pl.ds(pl.multiple_of((1 - odd) * last, EDGE), EDGE)], inner, sems.at[0])
    wide = outer.shape[0]
    last = image.shape[1] - wide
    to_outer = pltpu.make_async_copy(image.at[0, pl.ds(pl.multiple_of(odd * last, EDGE), wide)], outer, sems.at[1])
    to_outer.start(priority=1)
    to_inner.start(priority=1)
    to_inner.wait()
    to_outer.wait()


def edge_bands(taps_ref):
    e = lax.broadcasted_iota(jnp.int32, (2 * EDGE, 2 * EDGE), 0)
    k = lax.broadcasted_iota(jnp.int32, (2 * EDGE, 2 * EDGE), 1)
    upper = (e < EDGE) & (k < EDGE)
    lower = (e >= EDGE) & (k >= EDGE)
    return banded(taps_ref, jnp.where(upper, k - (EDGE - 2) - e, k + (EDGE + 2) - e), upper | lower)


def lens_kernel(taps_ref, image_ref, weight_ref, blocks_ref, edge_ref, bands_ref):
    x = image_ref[0]
    rows, cols = x.shape
    across = cols // B
    i = lax.broadcasted_iota(jnp.int32, (B, B), 0)
    j = lax.broadcasted_iota(jnp.int32, (B, B), 1)
    bands = banded(taps_ref, j - i + 2, None)
    columns = [shifted(x, b - 2) for b in range(5)]
    stack = jnp.concatenate([jnp.concatenate([c[:B] for c in columns], 0), jnp.concatenate([c[B:] for c in columns], 0)], 1)
    both = dot(bands, stack)
    main = both[:B] + both[B:]
    edges = edge_bands(taps_ref)
    bands_ref[...] = edges
    both = dot(edges, jnp.concatenate([c[B - EDGE : B + EDGE] for c in columns], 0))
    middle = both[: 2 * EDGE] + both[2 * EDGE :]
    corrected = jnp.concatenate(
        [
            main[: B - EDGE, :cols],
            main[B - EDGE :, :cols] + middle[EDGE:],
            main[:EDGE, cols:] + middle[:EDGE],
            main[EDGE:, cols:],
        ],
        0,
    )
    edge_ref[:EDGE] = corrected[:EDGE]
    edge_ref[EDGE:] = corrected[rows - EDGE :]
    weighted = (corrected * weight_ref[0].astype(F32)).astype(BF16)
    for k in range(rows // B * across):
        r, c = k // across * B, k % across * B
        blocks_ref[k] = weighted[r : r + B, c : c + B]


def pick_kernel(
    bands_ref, src, counts, inner_ref, outer_ref, edge_ref, weight_ref, blocks_ref, out, fixed_ref, src_ref, count_ref, sems
):
    loads = [pltpu.make_async_copy(src, src_ref, sems.at[0]), pltpu.make_async_copy(counts, count_ref, sems.at[1])]
    for load in loads:
        load.start()
    rows, cols = weight_ref.shape[1:]
    across = cols // B
    count = rows // B * across
    odd = lax.rem(lax.axis_index("tile"), 2) == 1
    inner, outer = inner_ref[...], outer_ref[...]
    rim = jnp.concatenate([jnp.where(odd, inner, outer[EDGE:]), jnp.where(odd, outer[:EDGE], inner)], 0)
    rims = jnp.concatenate([shifted(rim, b - 2) for b in range(5)], 0)
    both = dot(bands_ref[...], rims)
    for load in loads:
        load.wait()
    places = []
    for d in range(out.shape[0]):
        for q in range(out.shape[1]):
            live = q < count_ref[0, 0, d]
            block = src_ref[0, 0, q, d]
            out[d, q] = jnp.where(live, blocks_ref[block], jnp.zeros((), BF16))
            places.append((d, q, live, block))
    corrected = edge_ref[...] + (both[: 2 * EDGE] + both[2 * EDGE :])
    top = (corrected[:EDGE] * weight_ref[0, :EDGE].astype(F32)).astype(BF16)
    bottom = (corrected[EDGE:] * weight_ref[0, rows - EDGE :].astype(F32)).astype(BF16)
    for c in range(across):
        fixed_ref[c] = top[:, c * B : c * B + B]
        fixed_ref[count - across + c] = bottom[:, c * B : c * B + B]
    for d, q, live, block in places:
        at = pl.multiple_of(jnp.where(block < across, 0, B - EDGE), EDGE)
        out[d, q, pl.ds(at, EDGE), :] = jnp.where(live, fixed_ref[block], jnp.zeros((), BF16))


def strip_kernel(dst, in_ref, a_ref, rest_ref, acc_ref, dst_ref, sem):
    load = pltpu.make_async_copy(dst, dst_ref, sem)
    load.start()
    acc_ref[...] = jnp.zeros_like(acc_ref)
    load.wait()
    for d in range(in_ref.shape[0]):
        for q in range(in_ref.shape[1]):
            j = dst_ref[0, 0, q, d]
            acc_ref[j] = acc_ref[j] + in_ref[d, q].astype(F32)
    a_ref[...] = acc_ref[:EARLY].astype(BF16)
    rest_ref[...] = acc_ref[EARLY:]


def packed_rim(block):
    return jnp.concatenate([block[:H, :H], block[H:, :H]], 1)


def unpacked_rim(rim):
    gap = jnp.zeros((H, H), rim.dtype)
    return jnp.concatenate([jnp.concatenate([rim[:, :H], gap], 1), jnp.concatenate([rim[:, H:], gap], 1)], 0)


def rest_kernel(a_ref, rest_ref, anchor_ref, b_ref, first_ref, anchor_first_ref):
    b_ref[...] = rest_ref[...].astype(BF16)
    first_ref[...] = packed_rim(a_ref[0])
    anchor_first_ref[...] = packed_rim(anchor_ref[0])


def forward(blocks, right, left, middle):
    pairs = len(blocks) - 1
    both = jnp.concatenate([jnp.concatenate([blocks[m], blocks[m + 1]], 1) for m in range(pairs)], 0)
    p = dot(both, right).astype(BF16)
    re = [p[m * B : m * B + B, :B] for m in range(pairs)]
    im = [p[m * B : m * B + B, B:] for m in range(pairs)]
    spectra = dot(left, jnp.concatenate([jnp.concatenate(re, 1), jnp.concatenate(im, 1)], 0))
    p = dot(jnp.concatenate(blocks, 1), middle[: (pairs + 1) * B]).astype(BF16)
    return spectra, dot(left[:, :B], p)


def spectra_out(blocks, right_ref, left_ref, middle_ref, out_ref):
    spectra, rest = forward(blocks, right_ref[...], left_ref[...], middle_ref[...])
    out_ref[:, : spectra.shape[1]] = spectra.astype(BF16)
    out_ref[:, spectra.shape[1] :] = rest.astype(BF16)


def early_kernel(a_ref, *refs):
    spectra_out([a_ref[m] for m in range(EARLY)], *refs)


def late_kernel(a_ref, b_ref, rim_ref, *refs):
    spectra_out([a_ref[EARLY - 1]] + [b_ref[m] for m in range(b_ref.shape[0])] + [unpacked_rim(rim_ref[...])], *refs)


def correlate_chunk(cur_ref, blocks, tables, out, at, cross_ref, mag_ref, result_ref, sems):
    right, left, middle, back_left, back_right = (table[...] for table in tables)
    pairs = len(blocks) - 1
    lane = lax.broadcasted_iota(jnp.int32, (1, B), 1)
    twice = jnp.where(lane % H == 0, 1.0, 2.0)
    sums = []
    spectra, rest = forward(blocks, right, left, middle)
    for m in range(pairs + 1):
        f = spectra[:, m * B : m * B + B] if m < pairs else rest
        c = cur_ref[:, m * B : m * B + B].astype(F32)
        ar, ai, br, bi = c[:B], c[B:], f[:B], f[B:]
        re = ar * br + ai * bi
        im = ai * br - ar * bi
        square = re * re + im * im
        mag = square * lax.rsqrt(jnp.maximum(square, 1e-30))
        cross_ref[m, :B] = re
        cross_ref[m, B:] = im
        mag_ref[m] = mag
        total = jnp.sum(mag, axis=0, keepdims=True)
        sums.append(total * twice if m < pairs else total)
    row = lax.broadcasted_iota(jnp.int32, (pairs, B), 0)
    lanes = lax.broadcasted_iota(jnp.int32, (pairs, B), 1)
    mine = row == lanes % H
    table = jnp.concatenate(sums[:pairs], 0) + jnp.where(mine, sums[pairs], 0.0)
    aligned = lanes < H
    first = jnp.sum(jnp.where(aligned, table, 0.0), axis=1, keepdims=True)
    second = jnp.sum(jnp.where(aligned, 0.0, table), axis=1, keepdims=True)
    floor = jnp.where(aligned, first, second) * (0.1 / (B * B)) + 1e-6
    floor_middle = jnp.sum(jnp.where(mine, floor, 0.0), axis=0, keepdims=True)
    floor_middle = jnp.where(lane % H < pairs, floor_middle, 1.0)

    def whitened(m, low):
        scale = 1.0 / (mag_ref[m] + low)
        return jnp.concatenate([cross_ref[m, :B] * scale, cross_ref[m, B:] * scale], 0).astype(BF16)

    y_middle = dot(back_left[:B], whitened(pairs, floor_middle))
    y = dot(back_left, jnp.concatenate([whitened(m, floor[m : m + 1]) for m in range(pairs)], 1))
    is_zero = lane % H == 0
    both = []
    for m in range(pairs):
        turned = y_middle if m == 0 else pltpu.roll(y_middle, B - m, 1)
        imag = jnp.where(is_zero, turned, y[B:, m * B : m * B + B])
        both.append(jnp.concatenate([y[:B, m * B : m * B + B].astype(BF16), imag.astype(BF16)], 1))
    result = dot(jnp.concatenate(both, 0), back_right)
    sends = []
    for m in range(pairs):
        result_ref[2 * m] = result[m * B : m * B + B, :B]
        result_ref[2 * m + 1] = result[m * B : m * B + B, B:]
        sends.append(
            pltpu.make_async_copy(result_ref.at[pl.ds(2 * m, 2)], out.at[0, pl.ds(2 * (at + m), 2)], sems.at[m])
        )
        sends[-1].start()
    for send in sends:
        send.wait()


def correlate_early(cur_ref, a_ref, anchor_ref, *refs):
    is_first = lax.axis_index("sec") == 0
    blocks = [jnp.where(is_first, anchor_ref[m], a_ref[m]) for m in range(EARLY)]
    correlate_chunk(cur_ref, blocks, refs[:5], refs[5], 0, *refs[6:])


def correlate_late(held, cur_ref, a_ref, b_ref, rim_ref, anchor_ref, border_ref, *refs):
    del held
    is_first = lax.axis_index("sec") == 0
    blocks = [jnp.where(is_first, anchor_ref[EARLY - 1], a_ref[EARLY - 1])]
    blocks += [jnp.where(is_first, anchor_ref[EARLY + m], b_ref[m]) for m in range(b_ref.shape[0])]
    blocks += [unpacked_rim(jnp.where(is_first, border_ref[...], rim_ref[...]))]
    correlate_chunk(cur_ref, blocks, refs[:5], refs[5], EARLY - 1, *refs[6:])


SMEM = pl.BlockSpec(memory_space=pltpu.SMEM)
VMEM = pl.BlockSpec(memory_space=pltpu.VMEM)
ANY = pl.BlockSpec(memory_space=pl.ANY)
HBM = pl.BlockSpec(memory_space=pltpu.HBM)


def call(kernel, out_shape, in_specs, out_specs, scratch, flops, moved, args, aliases=None, grid=None, limit=VMEM_LIMIT):
    extra = {} if grid is None else {"grid": grid}
    return pl.pallas_call(
        kernel,
        out_shape=out_shape,
        in_specs=in_specs,
        out_specs=out_specs,
        scratch_shapes=scratch,
        input_output_aliases=aliases or {},
        compiler_params=pltpu.CompilerParams(vmem_limit_bytes=limit),
        cost_estimate=pl.CostEstimate(flops=flops, bytes_accessed=moved, transcendentals=0),
        **extra,
    )(*args)


def body(image, weight, lens_filter_taps, block_src, block_dst, valid_count, anchor):
    rows, cols = image.shape[1:]
    strips = lax.axis_size("tile")
    sections = lax.axis_size("sec")
    slots = block_src.shape[-1]
    count = anchor.shape[0]
    shape = jax.ShapeDtypeStruct
    block_src = block_src.transpose(0, 1, 3, 2)
    block_dst = block_dst.transpose(0, 2, 3, 1)
    whole = lambda *dims: pl.BlockSpec(dims, lambda i: (0,) * len(dims))
    back = [(i + 1, i) for i in range(strips - 1)]
    inner, outer = call(
        prepare_kernel,
        (shape((EDGE, cols), BF16), shape((2 * EDGE, cols), BF16)),
        [HBM],
        (VMEM,) * 2,
        [pltpu.SemaphoreType.DMA((2,))],
        2**33,
        2**17,
        (image,),
        limit=PREPARE_VMEM_LIMIT,
    )
    outer = lax.ppermute(outer, "tile", [(t, t + 2 * (t % 2) - 1) for t in range(1, strips - 1)])
    inner = lax.ppermute(inner, "tile", [(t, t ^ 1) for t in range(strips)])
    tile_blocks = rows // B * (cols // B)
    blocks, edge, bands = call(
        lens_kernel,
        (shape((tile_blocks, B, B), BF16), shape((2 * EDGE, cols), F32), shape((4 * EDGE, 10 * EDGE), BF16)),
        [VMEM, VMEM, VMEM],
        (VMEM, VMEM, VMEM),
        [],
        2**10,
        2**10,
        (lens_filter_taps, image, weight),
    )
    outgoing = call(
        pick_kernel,
        shape((strips, slots, B, B), BF16),
        [VMEM] * 8,
        VMEM,
        [
            pltpu.VMEM((tile_blocks, EDGE, B), BF16),
            pltpu.SMEM(block_src.shape, jnp.int32),
            pltpu.SMEM(valid_count.shape, jnp.int32),
            pltpu.SemaphoreType.DMA((2,)),
        ],
        2**20,
        4 * 2 * rows * cols,
        (bands, block_src, valid_count, inner, outer, edge, weight, blocks),
    )
    incoming = lax.all_to_all(outgoing, "tile", split_axis=0, concat_axis=0, tiled=True)
    part_a, rest = call(
        strip_kernel,
        (shape((EARLY, B, B), BF16), shape((count - EARLY, B, B), F32)),
        [VMEM, VMEM],
        (VMEM, VMEM),
        [pltpu.VMEM((count, B, B), F32), pltpu.SMEM(block_dst.shape, jnp.int32), pltpu.SemaphoreType.DMA],
        2**20,
        4 * 2 * rows * cols,
        (block_dst, incoming),
    )
    part_b, first, anchor_first = call(
        rest_kernel,
        (shape((count - EARLY, B, B), BF16), shape((H, B), BF16), shape((H, B), BF16)),
        [VMEM] * 3,
        (VMEM, VMEM, VMEM),
        [],
        2**18,
        6 * EARLY * B * B,
        (part_a, rest, anchor),
    )
    on = [(i, i + 1) for i in range(sections - 1)]
    prior_a = lax.ppermute(part_a, "sec", on)
    prior_b = lax.ppermute(part_b, "sec", on)
    own_rim = lax.ppermute(first, "tile", back)
    across = [(s * strips + d + 1, (s + 1) * strips + d) for s in range(sections - 1) for d in range(strips - 1)]
    prior_rim = lax.ppermute(first, ("sec", "tile"), across)
    border = lax.ppermute(anchor_first, "tile", back)
    right, left, middle, back_left, back_right = (jnp.asarray(t) for t in tables())
    early, late = EARLY - 1, count - EARLY + 1
    current = lambda kernel, pairs, *parts: call(
        kernel,
        shape((2 * B, (pairs + 1) * B), BF16),
        [VMEM] * (len(parts) + 3),
        VMEM,
        [],
        2**10,
        2**10,
        (*parts, right, left, middle),
    )
    spectra_a = current(early_kernel, early, part_a)
    spectra_b = current(late_kernel, late, part_a, part_b, own_rim)
    result = shape((1, 2 * count, B, B), F32)
    scratch = lambda pairs: [
        pltpu.VMEM((pairs + 1, 2 * B, B), F32),
        pltpu.VMEM((pairs + 1, B, B), F32),
        pltpu.VMEM((2 * pairs, B, B), F32),
        pltpu.SemaphoreType.DMA((pairs,)),
    ]
    held = call(
        correlate_early,
        result,
        [VMEM] * 8,
        HBM,
        scratch(early),
        2**10,
        2**10,
        (spectra_a, prior_a, anchor, right, left, middle, back_left, back_right),
    )
    return call(
        correlate_late,
        result,
        [HBM] + [VMEM] * 11,
        HBM,
        scratch(late),
        2**30,
        2**22,
        (held, spectra_b, prior_a, prior_b, prior_rim, anchor, border, right, left, middle, back_left, back_right),
        aliases={0: 0},
    )


def solution(mesh):
    in_specs = (
        P("sec", "tile", None),
        P("sec", "tile", None),
        P("sec", "tile", None),
        P("sec", "tile", None, None),
        P("sec", None, "tile", None),
        P("sec", "tile", None),
        P("tile", None, None),
    )
    out_specs = P("sec", "tile", None, None)
    return jax.shard_map(body, mesh=mesh, in_specs=in_specs, out_specs=out_specs, check_vma=False)
```
